256 devices in a mesh: mem: 8 (over z), dom: 32 (over y, x, core).
Axes of the slice: x: 4, y: 4, z: 8, core: 2. Of those that a mesh axis runs over, the one named last changes fastest.
Arguments:
- ensemble: float32 [80, 131072], P('mem', 'dom'), may hold values from -6 to 6
- obs_index: int32 [4, 4, 1024], replicated, may hold values from 0 to 131071
- obs_weight: float32 [4, 4, 1024], replicated, may hold values from 0.1 to 0.6
- obs_value: float32 [4, 1024], replicated, may hold values from -6 to 6
- obs_error_var: float32 [4, 1024], replicated, may hold values from 0.25 to 4
- loc_class: int32 [1024, 32], P(('dom', 'mem')), may hold values from 0 to 4
Outputs:
- posterior: float32 [80, 131072], P(None, ('dom', 'mem'))
The draws below stay inside these ranges and needn't reach their ends.
All inputs are finite; a program needn't handle non-finite values.
Results may differ from the reference program's by a relative error of at most 0.0085.
Values may be sent and summed in bfloat16 or wider, within the bound.
No kernel may reach another device: no remote copies, remote signals or barrier semaphores. Data moves between devices by JAX's collectives and lax.ppermute only.
A program may use at most 64 MiB of HBM per device.

```python
import math
import jax
import jax.numpy as jnp
from jax import lax

M = 80
NO = 1024
NB = 4
K = 4
VBLK = 128
NV = 131072
NOB = 8
NVB = 1024


def touch_ends(drawn, stream_key, smallest, top_value):
    extent = drawn.shape
    spot = [jax.random.randint(jax.random.fold_in(stream_key, axis), (), 0, extent[axis]) for axis in range(len(extent))]
    drawn = drawn.at[tuple(spot)].set(smallest)
    longest = extent.index(max(extent))
    spot[longest] = (spot[longest] + 1) % extent[longest]
    return drawn.at[tuple(spot)].set(top_value)


def level_of(own_key, extent, pieces, smallest, top_value):
    level = 1.0
    for axis_at, blocks in pieces:
        draws = jax.random.uniform(jax.random.fold_in(jax.random.fold_in(own_key, 6), axis_at), (blocks,), jnp.float32, smallest / len(pieces), top_value / len(pieces))
        level = level * jnp.repeat(jnp.exp(draws), extent[axis_at] // blocks).reshape((-1,) + (1,) * (len(extent) - 1 - axis_at))
    return level


def normal_values(rng, extent, spread, limit, split=(), kind=jnp.bfloat16):
    factor_of = level_of(rng, extent, split, -0.22, 0.18) if split else 1.0
    entries = jax.random.normal(rng, extent, jnp.float32) * spread * factor_of
    return jnp.minimum(jnp.maximum(entries, -limit), limit).astype(kind)


def setup_inputs(seed: int = 0) -> dict:
    seeds = jax.random.split(jax.random.key(seed), 7)
    return {
        "ensemble": normal_values(seeds[0], (M, NV), 1.0, 6.0, ((0, 8), (1, 32)), jnp.float32),
        "obs_index": touch_ends(jax.random.randint(seeds[1], (NB, K, NO), 0, NV), jax.random.fold_in(seeds[1], 1), 0, NV - 1).astype(jnp.int32),
        "obs_weight": jnp.clip(jax.random.uniform(seeds[2], (NB, K, NO), jnp.float32, 0.1, 0.6), 0.1, 0.6),
        "obs_value": normal_values(seeds[3], (NB, NO), 1.0, 6.0, (), jnp.float32),
        "obs_error_var": jnp.clip(jnp.exp(jax.random.uniform(seeds[4], (NB, NO), jnp.float32, math.log(0.25), math.log(4.0))), 0.25, 4.0),
        "loc_class": touch_ends(jax.random.randint(seeds[5], (NVB, NB * NOB), 0, 5), jax.random.fold_in(seeds[5], 1), 0, 4).astype(jnp.int32),
    }


EPS = 1e-05
LOC_TABLE = (1.0, 0.6848958, 0.2083333, 0.0164931, 0.0)
span_width = 512

def class_weights(classes):
    weights = jnp.zeros(classes.shape, jnp.float32)
    for level, value in enumerate(LOC_TABLE):
        weights = weights + jnp.where(classes == level, jnp.float32(value), jnp.float32(0.0))
    return weights

def adjust(prior, value, errvar):
    count = prior.shape[0]
    mean = lax.optimization_barrier(jnp.mean(prior, axis=0))
    anom = prior - mean
    var = lax.optimization_barrier(jnp.sum(anom * anom, axis=0)) / (count - 1)
    inverse = 1.0 / (var + EPS)
    post_var = 1.0 / (inverse + 1.0 / errvar)
    post_mean = post_var * (mean * inverse + value / errvar)
    shrink = jnp.sqrt(errvar / (errvar + var))
    incr = post_mean - mean + (shrink - 1.0) * anom
    return (anom, incr, inverse)

def update_block(block, classes, anom_b, incr_b, inverse):
    count = block.shape[0]
    centered = (block - lax.optimization_barrier(jnp.mean(block, axis=0))).astype(jnp.bfloat16)
    cov = lax.dot_general(centered, anom_b, (((0,), (0,)), ((), ())), preferred_element_type=jnp.float32) / (count - 1)
    weights = class_weights(classes)
    row_blocks, col_blocks = classes.shape
    scaled = (cov * inverse).reshape(row_blocks, cov.shape[0] // row_blocks, col_blocks, cov.shape[1] // col_blocks)
    gain = (scaled * weights[:, None, :, None]).reshape(cov.shape).astype(jnp.bfloat16)
    delta = lax.dot_general(incr_b, gain, (((1,), (1,)), ((), ())), preferred_element_type=jnp.float32)
    return block + delta

def reference(ensemble, obs_index, obs_weight, obs_value, obs_error_var, loc_class):
    members, total = ensemble.shape
    blocks = ensemble.reshape(members, total // span_width, span_width).transpose(1, 0, 2)
    obs_blocks = loc_class.shape[1] // NB
    rows_each = span_width // VBLK
    for batch in range(NB):
        index = obs_index[batch]
        picked = blocks[index // span_width, :, index % span_width]
        prior = lax.optimization_barrier(jnp.sum(picked * obs_weight[batch][:, :, None], axis=0)).T
        anom, incr, inverse = adjust(prior, obs_value[batch], obs_error_var[batch])
        anom_b = anom.astype(jnp.bfloat16)
        incr_b = incr.astype(jnp.bfloat16)
        classes = loc_class[:, batch * obs_blocks:(batch + 1) * obs_blocks]
        classes = classes.reshape(total // span_width, rows_each, obs_blocks)

        def step(pair):
            return update_block(pair[0], pair[1], anom_b, incr_b, inverse)
        blocks = lax.map(step, (blocks, classes))
    return blocks.transpose(1, 0, 2).reshape(members, total)
```

```python
import jax
import jax.numpy as jnp
from jax import lax
from jax.experimental import pallas as pl
from jax.experimental.pallas import tpu as pltpu
from jax.sharding import Mesh, PartitionSpec as P

EPS = 1e-05
LOC_TABLE = (1.0, 0.6848958, 0.2083333, 0.0164931, 0.0)
F32 = jnp.float32
BF16 = jnp.bfloat16
VMEM = pl.BlockSpec(memory_space=pltpu.VMEM)
SMEM = pl.BlockSpec(memory_space=pltpu.SMEM)
PARAMS = pltpu.CompilerParams(vmem_limit_bytes=40 * 2**20)

CHUNK = 168
PACK = 176


def call(body, shapes, args, scalars, scratch=(), flops=0, name=None):
    outs = [jax.ShapeDtypeStruct(s, d) for s, d in shapes]
    moved = sum(a.size * a.dtype.itemsize for a in args) + sum(o.size * o.dtype.itemsize for o in outs)
    return pl.pallas_call(
        body,
        out_shape=outs,
        in_specs=[SMEM] * len(scalars) + [VMEM] * len(args),
        out_specs=[VMEM] * len(outs),
        scratch_shapes=list(scratch),
        compiler_params=PARAMS,
        cost_estimate=pl.CostEstimate(flops=flops, bytes_accessed=moved, transcendentals=0),
        name=name,
    )(*scalars, *args)


def lanes(info_ref):
    return pl.ds(pl.multiple_of(info_ref[1] * 128, 128), 128)


def collect(info_ref, index_ref, ens_ref, class_ref, out_ref, ext_ref, row_ref):
    ext_ref[0:8, :] = ens_ref[0:8, :]
    for r in range(4):
        ext_ref[8 + 2 * r : 10 + 2 * r, :] = ens_ref[8:10, :]
    for i in range(4):
        row_ref[0:1, 32 * i : 32 * i + 32] = class_ref[i : i + 1, :].astype(F32)
    row = jnp.broadcast_to(row_ref[...], (8, 128))
    first = info_ref[0]

    def group(g, carry):
        for k in range(4):
            local = [index_ref[b, k : k + 1, pl.ds(pl.multiple_of(g * 128, 128), 128)] - first for b in range(4)]
            tail = jnp.concatenate([jnp.broadcast_to(v, (2, 128)) for v in local], axis=0)
            wide = [jnp.broadcast_to(v, (8, 128)) for v in local] + [tail]
            for b in range(5):
                low = wide[b] & 127
                high = wide[b] >> 7
                top = 0 if b < 4 else 8
                acc = jnp.zeros((8, 128), F32)
                for block in range(32):
                    source = ext_ref[top : top + 8, block * 128 : (block + 1) * 128]
                    got = jnp.take_along_axis(source, low, axis=1)
                    acc = jnp.where(high == block, got, acc)
                out_ref[g, 40 * k + 8 * b : 40 * k + 8 * b + 8, :] = acc
        out_ref[g, 160:168, :] = row
        return carry

    lax.fori_loop(0, 8, group, 0)


def add_sources(recv_ref, out_ref):
    total = recv_ref[0, 0:160, :]
    for s in range(1, 8):
        total = total + recv_ref[s, 0:160, :]
    out_ref[0:160, :] = total
    for s in range(8):
        out_ref[160 + s : 161 + s, :] = recv_ref[s, 160:161, :]


def add_rows(info_ref, weight_ref, p0_ref, p1_ref, p2_ref, p3_ref, out_ref, sum_ref):
    parts = [p0_ref, p1_ref, p2_ref, p3_ref]
    sum_ref[...] = (p0_ref[0:160, :] + p1_ref[0:160, :]) + (p2_ref[0:160, :] + p3_ref[0:160, :])
    here = lanes(info_ref)
    head = jnp.zeros((8, 128), F32)
    tail = jnp.zeros((2, 128), F32)
    for k in range(4):
        weight = weight_ref[0, k : k + 1, here]
        head = head + sum_ref[40 * k : 40 * k + 8, :] * weight
        tail = tail + sum_ref[40 * k + 32 : 40 * k + 34, :] * weight
        out_ref[32 * k : 32 * k + 24, :] = sum_ref[40 * k + 8 : 40 * k + 32, :]
        out_ref[32 * k + 24 : 32 * k + 32, :] = jnp.zeros((8, 128), F32)
        out_ref[32 * k + 24 : 32 * k + 30, :] = sum_ref[40 * k + 34 : 40 * k + 40, :]
    out_ref[128:136, :] = head
    out_ref[136:144, :] = jnp.zeros((8, 128), F32)
    out_ref[136:138, :] = tail
    for s in range(4):
        place = lax.rem(info_ref[2] - s + 4, 4) * 8 + 144
        out_ref[pl.ds(pl.multiple_of(place, 8), 8), :] = parts[s][160:168, :]


def increments(prior, value, errvar, anom_ref):
    mean = jnp.mean(prior, axis=0, keepdims=True)
    anom = prior - mean
    var = jnp.sum(anom * anom, axis=0, keepdims=True) / 79.0
    inverse = 1.0 / (var + EPS)
    post_var = 1.0 / (inverse + 1.0 / errvar)
    post_mean = post_var * (mean * inverse + value / errvar)
    shrink = jnp.sqrt(errvar / (errvar + var))
    incr = post_mean - mean + (shrink - 1.0) * anom
    scaled = incr.astype(BF16).astype(F32) * (inverse / 79.0)
    high = scaled.astype(BF16)
    low = (scaled - high.astype(F32)).astype(BF16)
    anom_ref[80:128, :] = jnp.zeros((48, 128), BF16)
    anom_ref[0:80, :] = anom.astype(BF16)
    dims = (((1,), (1,)), ((), ()))
    anom_b = anom_ref[...]
    return lax.dot_general(high, anom_b, dims, preferred_element_type=F32) + lax.dot_general(
        low, anom_b, dims, preferred_element_type=F32
    )


def first_batch(info_ref, pack_ref, value_ref, errvar_ref, out_ref, prior_ref, anom_ref):
    for z in range(8):
        prior_ref[8 * z : 8 * z + 8, :] = pack_ref[z, 128:136, :]
        prior_ref[64 + 2 * z : 66 + 2 * z, :] = pack_ref[z, 136:138, :]
    here = lanes(info_ref)
    out_ref[...] = increments(prior_ref[...], value_ref[0:1, here], errvar_ref[0:1, here], anom_ref)


def unpack(info_ref, pack_ref, index_ref, x1_ref, x2_ref, x3_ref, loc_ref):
    here = lanes(info_ref)
    table = pack_ref[:, 144:176, :].reshape(256, 128).astype(BF16)
    outs = [x1_ref, x2_ref, x3_ref]
    for b in range(3):
        for k in range(4):
            at = slice(128 * k, 128 * k + 128)
            for z in range(8):
                outs[b][8 * z : 8 * z + 8, at] = pack_ref[z, 32 * k + 8 * b : 32 * k + 8 * b + 8, :]
                outs[b][64 + 2 * z : 66 + 2 * z, at] = pack_ref[z, 32 * k + 24 + 2 * b : 32 * k + 26 + 2 * b, :]
            block = index_ref[b + 1, k : k + 1, here] >> 7
            holder = ((block >> 2) & 7) * 32 + (block >> 5)
            own = (lax.broadcasted_iota(jnp.int32, (256, 128), 0) == holder).astype(F32).astype(BF16)
            found = lax.dot_general(table, own, (((0,), (0,)), ((), ())), preferred_element_type=F32)
            which = block & 3
            level = jnp.zeros((32, 128), F32)
            for i in range(4):
                level = level + jnp.where(which == i, found[32 * i : 32 * i + 32, :], 0.0)
            weights = jnp.zeros((32, 128), F32)
            for n, w in enumerate(LOC_TABLE):
                weights = weights + jnp.where(level == n, w, 0.0)
            loc_ref[b, :, at] = weights


def slots(info_ref):
    here, core = info_ref[3], info_ref[4]
    straight = [lax.rem(here - s + 4, 4) * 2 + core for s in range(4)]
    return straight + [lax.rem(here - s + 4, 4) * 2 + 1 - core for s in range(4)]


def stack(info_ref, g_refs, stack_ref):
    for slot, g_ref in zip(slots(info_ref), g_refs):
        whole = g_ref[...]
        high = whole.astype(BF16)
        rows = pl.ds(pl.multiple_of(slot * 80, 16), 80)
        stack_ref[rows, 0:128] = high
        stack_ref[rows, 128:256] = (whole - high.astype(F32)).astype(BF16)


def doubled(x, twice_ref):
    centered = (x - jnp.mean(x, axis=0, keepdims=True)).astype(BF16)
    width = x.shape[1]
    for top in (0, 128):
        twice_ref[top : top + 80, 0:width] = centered
        twice_ref[top + 80 : top + 128, 0:width] = jnp.zeros((48, width), BF16)


def moved(x, loc, stack_ref, twice_ref, all_ref):
    doubled(x, twice_ref)
    all_ref[...] = jnp.dot(stack_ref[...], twice_ref[...], preferred_element_type=F32)
    total = all_ref[0:80, :] * loc[0:1, :]
    for ob in range(1, 8):
        total = total + all_ref[80 * ob : 80 * ob + 80, :] * loc[ob : ob + 1, :]
    return x + total


def next_batch(batch):
    def body(info_ref, *refs):
        g_refs = refs[:8]
        x_ref, loc_ref, weight_ref, value_ref, errvar_ref, out_ref, stack_ref, twice_ref, all_ref, anom_ref = refs[8:]
        stack(info_ref, g_refs, stack_ref)
        x = moved(x_ref[...], loc_ref[batch - 1, 8 * batch - 8 : 8 * batch, :], stack_ref, twice_ref, all_ref)
        here = lanes(info_ref)
        prior = x[:, 0:128] * weight_ref[batch, 0:1, here]
        for k in range(1, 4):
            prior = prior + x[:, 128 * k : 128 * k + 128] * weight_ref[batch, k : k + 1, here]
        out_ref[...] = increments(prior, value_ref[batch : batch + 1, here], errvar_ref[batch : batch + 1, here], anom_ref)

    return body


def later(batch, count):
    def body(info_ref, class_ref, *refs):
        g_refs = refs[:8]
        refs = refs[8:]
        x_refs, loc_ref, state_ref = refs[:count], refs[count], refs[count + 1]
        refs = refs[count + 2 :]
        out_refs, state_out_ref = refs[:count], refs[count]
        stack_ref, twice_ref, all_ref, work_ref = refs[count + 1 :]
        if count:
            stack(info_ref, g_refs, stack_ref)
        for n in range(count):
            b = 3 - count + n
            loc = loc_ref[b, 8 * batch : 8 * batch + 8, :]
            out_refs[n][...] = moved(x_refs[n][...], loc, stack_ref, twice_ref, all_ref)
        if batch == 0:
            for z in range(8):
                work_ref[8 * z : 8 * z + 8, :] = state_ref[10 * z : 10 * z + 8, :]
                work_ref[64 + 2 * z : 66 + 2 * z, :] = state_ref[10 * z + 8 : 10 * z + 10, :]
        else:
            work_ref[...] = state_ref[...]
        state = work_ref[...]
        doubled(state, twice_ref)
        places = slots(info_ref)
        for block in range(4):
            total = jnp.zeros((80, 128), F32)
            for slot, g_ref in zip(places, g_refs):
                level = class_ref[block, 8 * batch + slot]
                weight = jnp.float32(0.0)
                for n, w in enumerate(LOC_TABLE):
                    weight = jnp.where(level == n, jnp.float32(w), weight)
                total = total + g_ref[...] * weight
            high = total.astype(BF16)
            low = (total - high.astype(F32)).astype(BF16)
            both = jnp.concatenate([high, low], axis=1)
            at = slice(128 * block, 128 * block + 128)
            work_ref[:, at] = state[:, at] + jnp.dot(both, twice_ref[:, at], preferred_element_type=F32)
        if batch == 3:
            for z in range(8):
                state_out_ref[10 * z : 10 * z + 8, :] = work_ref[8 * z : 8 * z + 8, :]
                state_out_ref[10 * z + 8 : 10 * z + 10, :] = work_ref[64 + 2 * z : 66 + 2 * z, :]
        else:
            state_out_ref[...] = work_ref[...]

    return body


def shift(a, axis, by, size):
    return lax.ppermute(a, axis, [(i, (i + by) % size) for i in range(size)])


def spread(g):
    own = [g] + [shift(g, "x", s, 4) for s in (1, 2, 3)]
    return own + [shift(v, "c", 1, 2) for v in own]


def per_device(ensemble, obs_index, obs_weight, obs_value, obs_error_var, loc_class):
    z, y, x, c = [lax.axis_index(n) for n in ("z", "y", "x", "c")]
    block = x * 2 + c
    info = jnp.stack([(y * 8 + block) * 4096, block, y, x, c]).astype(jnp.int32)

    everyone = lax.all_gather(ensemble, "z", tiled=True)

    (sent,) = call(
        collect,
        [((8, CHUNK, 128), F32)],
        [obs_index, ensemble, loc_class],
        [info],
        [pltpu.VMEM((16, 4096), F32), pltpu.VMEM((1, 128), F32)],
        name="collect",
    )
    got = lax.all_to_all(sent.reshape(8 * CHUNK, 128), ("x", "c"), 0, 0, tiled=True)
    (part,) = call(add_sources, [((CHUNK, 128), F32)], [got.reshape(8, CHUNK, 128)], [], name="add_sources")
    parts = [part] + [shift(part, "y", s, 4) for s in (1, 2, 3)]
    (pack,) = call(
        add_rows, [((PACK, 128), F32)], [obs_weight] + parts, [info], [pltpu.VMEM((160, 128), F32)], name="add_rows"
    )
    pack = lax.all_gather(pack, "z")

    anom = pltpu.VMEM((128, 128), BF16)
    (g,) = call(
        first_batch,
        [((80, 128), F32)],
        [pack, obs_value, obs_error_var],
        [info],
        [pltpu.VMEM((80, 128), F32), anom],
        name="first_batch",
    )
    work = [pltpu.VMEM((640, 256), BF16), pltpu.VMEM((256, 512), BF16), pltpu.VMEM((640, 512), F32)]
    *xs, loc = call(
        unpack,
        [((80, 512), F32)] * 3 + [((3, 32, 512), F32)],
        [pack, obs_index],
        [info],
        flops=2 * 256 * 128 * 1536,
        name="unpack",
    )
    state = lax.dynamic_slice(everyone, (0, z * 512), (80, 512))
    for batch in range(4):
        gs = spread(g)
        if batch < 3:
            (g,) = call(
                next_batch(batch + 1),
                [((80, 128), F32)],
                gs + [xs[0], loc, obs_weight, obs_value, obs_error_var],
                [info],
                work + [anom],
                flops=2 * 640 * 256 * 512,
                name="next_batch",
            )
        xs = xs[1:]
        *xs, state = call(
            later(batch, len(xs)),
            [((80, 512), F32)] * (len(xs) + 1),
            gs + list(xs) + [loc, state],
            [info, loc_class],
            work + [pltpu.VMEM((80, 512), F32)],
            flops=2 * 640 * 256 * 512 * (len(xs) + 1),
            name="later",
        )
    return state


def solution(mesh):
    fine = Mesh(mesh.devices.reshape(8, 4, 4, 2), ("z", "y", "x", "c"))
    tiles = ("y", "x", "c")
    in_specs = (P("z", tiles), P(), P(), P(), P(), P(tiles + ("z",), None))
    out_specs = P(None, tiles + ("z",))
    return jax.shard_map(per_device, mesh=fine, in_specs=in_specs, out_specs=out_specs, check_vma=False)
```

```python
import jax
import jax.numpy as jnp
from jax import lax
from jax.experimental import pallas as pl
from jax.experimental.pallas import tpu as pltpu
from jax.sharding import Mesh, PartitionSpec as P

EPS = 1e-05
LOC_TABLE = (1.0, 0.6848958, 0.2083333, 0.0164931, 0.0)
F32 = jnp.float32
BF16 = jnp.bfloat16
VMEM = pl.BlockSpec(memory_space=pltpu.VMEM)
SMEM = pl.BlockSpec(memory_space=pltpu.SMEM)

CHUNK = 168
PACK = 192


def call(body, shapes, args, scalars, scratch=(), flops=0, name=None):
    outs = [jax.ShapeDtypeStruct(s, d) for s, d in shapes]
    moved = sum(a.size * a.dtype.itemsize for a in args) + sum(o.size * o.dtype.itemsize for o in outs)
    made = pl.pallas_call(
        body,
        out_shape=outs,
        in_specs=[SMEM] * len(scalars) + [VMEM] * len(args),
        out_specs=[VMEM] * len(outs),
        scratch_shapes=list(scratch),
        compiler_params=pltpu.CompilerParams(vmem_limit_bytes=40 * 2**20),
        cost_estimate=pl.CostEstimate(flops=flops, bytes_accessed=moved, transcendentals=0),
        name=name,
    )(*scalars, *args)
    return list(made)


def lanes(info_ref):
    return pl.ds(pl.multiple_of(info_ref[1] * 128, 128), 128)


def pick(info_ref, shifts, core, index_ref, ext_ref, tile, start_ref, out_refs):
    first = info_ref[0]

    def group(n, carry):
        by = shifts + n
        block = lax.rem(info_ref[3] + by, 4) * 2 + core
        here = pl.ds(pl.multiple_of(block * 128, 128), 128)
        for k in range(4):
            local = [index_ref[b, k : k + 1, here] - first for b in range(4)]
            tail = jnp.concatenate([jnp.broadcast_to(v, (2, 128)) for v in local], axis=0)
            wide = [jnp.broadcast_to(v, (8, 128)) for v in local] + [tail]
            for b in range(5):
                low = wide[b] & 127
                high = wide[b] >> 7
                top = 0 if b < 4 else 8
                rows = slice(40 * k + 8 * b, 40 * k + 8 * b + 8)
                acc = jnp.zeros((8, 128), F32) if start_ref is None else start_ref[lax.rem(by, 4), rows, :]
                for part in range(32):
                    source = ext_ref[top : top + 8, part * 128 : (part + 1) * 128]
                    got = jnp.take_along_axis(source, low, axis=1)
                    acc = jnp.where(high == part, got, acc)
                out_refs[n, rows, :] = acc
        rest = tile if start_ref is None else tile + start_ref[lax.rem(by, 4), 160:168, :]
        out_refs[n, 160:168, :] = rest
        return carry

    lax.fori_loop(0, out_refs.shape[0], group, 0)


def collect_other(info_ref, index_ref, ens_ref, class_ref, out_ref, ext_ref, tile_ref, row_ref):
    ext_ref[0:8, :] = ens_ref[0:8, :]
    for r in range(4):
        ext_ref[8 + 2 * r : 10 + 2 * r, :] = ens_ref[8:10, :]
    even = lax.broadcasted_iota(jnp.int32, (32, 16), 0) == 2 * lax.broadcasted_iota(jnp.int32, (32, 16), 1)
    odd = lax.broadcasted_iota(jnp.int32, (32, 16), 0) == 2 * lax.broadcasted_iota(jnp.int32, (32, 16), 1) + 1
    mix = jnp.where(even, 1.0, jnp.where(odd, 8.0, 0.0)).astype(BF16)
    pairs = jnp.dot(class_ref[...].astype(F32).astype(BF16), mix, preferred_element_type=F32)
    for half in range(2):
        for i in range(4):
            row_ref[0:1, 64 * half + 16 * i : 64 * half + 16 * i + 16] = pairs[i : i + 1, :]
    row = lax.broadcasted_iota(jnp.int32, (8, 128), 0) == (info_ref[2] & 1) * 4 + info_ref[3]
    lane = (lax.broadcasted_iota(jnp.int32, (8, 128), 1) >> 6) == info_ref[4]
    tile = jnp.where(row & lane, jnp.broadcast_to(row_ref[...], (8, 128)), 0.0)
    tile_ref[...] = tile
    pick(info_ref, 0, 1 - info_ref[4], index_ref, ext_ref, tile, None, out_ref)


def collect_own(info_ref, index_ref, ext_ref, tile_ref, out_ref):
    pick(info_ref, 1, info_ref[4], index_ref, ext_ref, tile_ref[...], None, out_ref)


def collect_rest(info_ref, index_ref, ext_ref, tile_ref, start_ref, p0_ref, p3_ref, work_ref):
    pick(info_ref, 3, info_ref[4], index_ref, ext_ref, tile_ref[...], start_ref, work_ref)
    p3_ref[...] = work_ref[0]
    p0_ref[...] = work_ref[1]


def add_cores(own_ref, other_ref, p1_ref, p2_ref):
    p1_ref[...] = own_ref[0] + other_ref[1]
    p2_ref[...] = own_ref[1] + other_ref[2]


def add_columns(p0_ref, p1_ref, p2_ref, p3_ref, out_ref):
    out_ref[...] = (p0_ref[...] + p1_ref[...]) + (p2_ref[...] + p3_ref[...])


def add_rows(info_ref, weight_ref, ext_ref, p0_ref, p1_ref, p2_ref, p3_ref, out_ref, sum_ref):
    parts = [p0_ref, p1_ref, p2_ref, p3_ref]
    sum_ref[...] = (p0_ref[0:160, :] + p1_ref[0:160, :]) + (p2_ref[0:160, :] + p3_ref[0:160, :])
    here = lanes(info_ref)
    head = jnp.zeros((8, 128), F32)
    tail = jnp.zeros((2, 128), F32)
    for k in range(4):
        weight = weight_ref[0, k : k + 1, here]
        head = head + sum_ref[40 * k : 40 * k + 8, :] * weight
        tail = tail + sum_ref[40 * k + 32 : 40 * k + 34, :] * weight
    classes = [jnp.zeros((8, 128), F32)] * 2
    for s in range(4):
        upper = lax.rem(info_ref[2] - s + 4, 4) >> 1
        for t in range(2):
            classes[t] = classes[t] + jnp.where(upper == t, parts[s][160:168, :], 0.0)
    pair = lax.broadcasted_iota(jnp.int32, (8, 128), 0) >> 1
    for z in range(8):
        for k in range(4):
            out_ref[z, 24 * k : 24 * k + 24, :] = sum_ref[40 * k + 8 : 40 * k + 32, :]
            out_ref[z, 104 + 6 * k : 110 + 6 * k, :] = sum_ref[40 * k + 34 : 40 * k + 40, :]
        out_ref[z, 96:104, :] = head
        out_ref[z, 128:136, :] = jnp.zeros((8, 128), F32)
        out_ref[z, 128:130, :] = tail
        last = jnp.zeros((8, 128), F32)
        for i in range(4):
            at = slice(512 * z + 128 * i, 512 * z + 128 * i + 128)
            out_ref[z, 136 + 8 * i : 144 + 8 * i, :] = ext_ref[0:8, at]
            last = jnp.where(pair == i, ext_ref[8:16, at], last)
        out_ref[z, 168:176, :] = last
        for t in range(2):
            out_ref[z, 176 + 8 * t : 184 + 8 * t, :] = classes[t]


def increments(prior, value, errvar, out_ref, wide_ref):
    mean = jnp.mean(prior, axis=0, keepdims=True)
    anom = prior - mean
    var = jnp.sum(anom * anom, axis=0, keepdims=True) / 79.0
    inverse = 1.0 / (var + EPS)
    post_var = 1.0 / (inverse + 1.0 / errvar)
    post_mean = post_var * (mean * inverse + value / errvar)
    shrink = jnp.sqrt(errvar / (errvar + var))
    incr = post_mean - mean + (shrink - 1.0) * anom
    rest = inverse / 79.0
    wide_ref[0:80, :] = anom.astype(BF16).astype(F32)
    wide_ref[80:128, :] = jnp.zeros((48, 128), F32)
    for row in (80, 81, 82):
        part = rest.astype(BF16).astype(F32)
        wide_ref[row : row + 1, :] = part
        rest = rest - part
    out_ref[0:128, :] = jnp.transpose(wide_ref[...]).astype(BF16)
    out_ref[128:208, :] = incr.astype(BF16)


def first_batch(info_ref, pack_ref, value_ref, errvar_ref, out_ref, prior_ref, wide_ref):
    for z in range(8):
        prior_ref[8 * z : 8 * z + 8, :] = pack_ref[z, 96:104, :]
        prior_ref[64 + 2 * z : 66 + 2 * z, :] = pack_ref[z, 128:130, :]
    here = lanes(info_ref)
    increments(prior_ref[...], value_ref[0:1, here], errvar_ref[0:1, here], out_ref, wide_ref)


def center(x, out_ref):
    out_ref[0:80, :] = (x - jnp.mean(x, axis=0, keepdims=True)).astype(BF16)
    out_ref[80:128, :] = jnp.zeros((48, x.shape[1]), BF16)


def unpack(info_ref, pack_ref, index_ref, *refs):
    outs, centered, loc_ref = refs[:4], refs[4:8], refs[8]
    here = lanes(info_ref)
    table = pack_ref[:, 176:192, :].reshape(128, 128).astype(BF16)
    for b in range(4):
        for k in range(4):
            at = slice(128 * k, 128 * k + 128)
            for z in range(8):
                if b < 3:
                    outs[b][8 * z : 8 * z + 8, at] = pack_ref[z, 24 * k + 8 * b : 24 * k + 8 * b + 8, :]
                    outs[b][64 + 2 * z : 66 + 2 * z, at] = pack_ref[z, 104 + 6 * k + 2 * b : 106 + 6 * k + 2 * b, :]
                else:
                    outs[b][8 * z : 8 * z + 8, at] = pack_ref[z, 136 + 8 * k : 144 + 8 * k, :]
                    outs[b][64 + 2 * z : 66 + 2 * z, at] = pack_ref[z, 168 + 2 * k : 170 + 2 * k, :]
            if b < 3:
                block = index_ref[b + 1, k : k + 1, here] >> 7
            else:
                block = jnp.full((1, 128), info_ref[5] + k, jnp.int32)
            holder = ((block >> 2) & 7) * 16 + (block >> 6)
            own = (lax.broadcasted_iota(jnp.int32, (128, 128), 0) == holder).astype(F32).astype(BF16)
            found = lax.dot_general(table, own, (((0,), (0,)), ((), ())), preferred_element_type=F32)
            which = ((block >> 5) & 1) * 4 + (block & 3)
            pairs = jnp.zeros((16, 128), F32)
            for i in range(8):
                pairs = pairs + jnp.where(which == i, found[16 * i : 16 * i + 16, :], 0.0)
            odd = jnp.floor(pairs * 0.125)
            for top, level in ((0, pairs - 8.0 * odd), (16, odd)):
                weights = jnp.zeros((16, 128), F32)
                for n, w in enumerate(LOC_TABLE):
                    weights = weights + jnp.where(level == n, w, 0.0)
                loc_ref[b, top : top + 16, at] = weights
    for x_ref, c_ref in zip(outs, centered):
        center(x_ref[...], c_ref)


def slots(info_ref):
    here, core = info_ref[3], info_ref[4]
    straight = [lax.rem(here - s + 4, 4) * 2 + core for s in range(4)]
    return straight + [lax.rem(here - s + 4, 4) * 2 + 1 - core for s in range(4)]


def stack(info_ref, refs, anom_ref, incr_ref, inverse_ref):
    for slot, ref in zip(slots(info_ref), refs):
        at = pl.ds(pl.multiple_of(slot * 128, 128), 128)
        rows = ref[0:128, :]
        anom_ref[at, :] = rows
        incr_ref[:, at] = ref[128:208, :]
        wide = rows.astype(F32)
        inverse_ref[at, :] = jnp.broadcast_to((wide[:, 80:81] + wide[:, 81:82]) + wide[:, 82:83], (128, 128))


def moved(x_ref, centered_ref, loc_ref, at, batch, anom_ref, incr_ref, inverse_ref, cov_ref, gain_ref):
    cov_ref[...] = jnp.dot(anom_ref[...], centered_ref[...], preferred_element_type=F32)
    for ob in range(8):
        row = 16 * (ob % 2) + 4 * batch + ob // 2
        rows = slice(128 * ob, 128 * ob + 128)
        for k in range(4):
            cols = slice(128 * k, 128 * k + 128)
            gain = (cov_ref[rows, cols] * inverse_ref[rows, :]) * loc_ref[at, row : row + 1, cols]
            gain_ref[rows, cols] = gain.astype(BF16)
    return x_ref[...] + jnp.dot(incr_ref[...], gain_ref[...], preferred_element_type=F32)


def next_batch(batch):
    def body(info_ref, *refs):
        x_ref, c_ref, loc_ref, weight_ref, value_ref, errvar_ref = refs[8:14]
        out_ref, anom_ref, incr_ref, inverse_ref, cov_ref, gain_ref, wide_ref = refs[14:]
        stack(info_ref, refs[:8], anom_ref, incr_ref, inverse_ref)
        x = moved(x_ref, c_ref, loc_ref, batch - 1, batch - 1, anom_ref, incr_ref, inverse_ref, cov_ref, gain_ref)
        here = lanes(info_ref)
        prior = x[:, 0:128] * weight_ref[batch, 0:1, here]
        for k in range(1, 4):
            prior = prior + x[:, 128 * k : 128 * k + 128] * weight_ref[batch, k : k + 1, here]
        increments(prior, value_ref[batch : batch + 1, here], errvar_ref[batch : batch + 1, here], out_ref, wide_ref)

    return body


def advance(at, batch):
    def body(anom_ref, incr_ref, inverse_ref, x_ref, c_ref, loc_ref, out_ref, c_out_ref, cov_ref, gain_ref):
        x = moved(x_ref, c_ref, loc_ref, at, batch, anom_ref, incr_ref, inverse_ref, cov_ref, gain_ref)
        out_ref[...] = x
        center(x, c_out_ref)

    return body


def finish(info_ref, *refs):
    x_ref, c_ref, loc_ref, out_ref, anom_ref, incr_ref, inverse_ref, cov_ref, gain_ref, work_ref = refs[8:]
    stack(info_ref, refs[:8], anom_ref, incr_ref, inverse_ref)
    work_ref[...] = moved(x_ref, c_ref, loc_ref, 3, 3, anom_ref, incr_ref, inverse_ref, cov_ref, gain_ref)
    for z in range(8):
        out_ref[10 * z : 10 * z + 8, :] = work_ref[8 * z : 8 * z + 8, :]
        out_ref[10 * z + 8 : 10 * z + 10, :] = work_ref[64 + 2 * z : 66 + 2 * z, :]


def shift(a, axis, by, size):
    return lax.ppermute(a, axis, [(i, (i + by) % size) for i in range(size)])


def spread(g):
    own = [g] + [shift(g, "x", s, 4) for s in (1, 2, 3)]
    return own + [shift(v, "c", 1, 2) for v in own]


def per_device(ensemble, obs_index, obs_weight, obs_value, obs_error_var, loc_class):
    z, y, x, c = [lax.axis_index(n) for n in ("z", "y", "x", "c")]
    block = x * 2 + c
    info = jnp.stack([(y * 8 + block) * 4096, block, y, x, c, (y * 8 + block) * 32 + z * 4]).astype(jnp.int32)

    rows = [((CHUNK, 128), F32)]
    other, ext, tile = call(
        collect_other,
        [((4, CHUNK, 128), F32), ((16, 4096), F32), ((8, 128), F32)],
        [obs_index, ensemble, loc_class],
        [info],
        [pltpu.VMEM((1, 128), F32)],
        name="collect_other",
    )
    other = shift(other, "c", 1, 2)
    (own,) = call(collect_own, [((2, CHUNK, 128), F32)], [obs_index, ext, tile], [info], flops=10**9, name="collect_own")
    p1, p2 = call(add_cores, rows * 2, [own, other], [], name="add_cores")
    p1, p2 = shift(p1, "x", 1, 4), shift(p2, "x", 2, 4)
    p0, p3 = call(
        collect_rest,
        rows * 2,
        [obs_index, ext, tile, other],
        [info],
        [pltpu.VMEM((2, CHUNK, 128), F32)],
        flops=10**9,
        name="collect_rest",
    )
    sums = [p0, p1, p2, shift(p3, "x", 3, 4)]
    (part,) = call(add_columns, rows, sums, [], name="add_columns")
    parts = [part] + [shift(part, "y", s, 4) for s in (1, 2, 3)]
    (pack,) = call(
        add_rows,
        [((8, PACK, 128), F32)],
        [obs_weight, ext] + parts,
        [info],
        [pltpu.VMEM((160, 128), F32)],
        name="add_rows",
    )
    pack = lax.all_to_all(pack, "z", 0, 0, tiled=True)

    tall, centered, sent = ((80, 512), F32), ((128, 512), BF16), ((208, 128), BF16)
    blocks = [((1024, 128), BF16), ((80, 1024), BF16), ((1024, 128), F32)]
    wide = pltpu.VMEM((128, 128), F32)
    work = [pltpu.VMEM((1024, 512), F32), pltpu.VMEM((1024, 512), BF16)]
    flops = 2 * 2 * 1024 * 128 * 512
    (g,) = call(
        first_batch,
        [sent],
        [pack, obs_value, obs_error_var],
        [info],
        [pltpu.VMEM((80, 128), F32), wide],
        name="first_batch",
    )
    *both, loc = call(
        unpack,
        [tall] * 4 + [centered] * 4 + [((4, 32, 512), F32)],
        [pack, obs_index],
        [info],
        flops=2 * 128 * 128 * 2048,
        name="unpack",
    )
    held = dict(enumerate(zip(both[:4], both[4:])))
    for batch in range(3):
        g, *stacked = call(
            next_batch(batch + 1),
            [sent] + blocks,
            spread(g) + [*held[batch], loc, obs_weight, obs_value, obs_error_var],
            [info],
            work + [wide],
            flops=flops,
            name="next_batch",
        )
        for at in range(batch + 1, 4):
            held[at] = call(
                advance(at, batch),
                [tall, centered],
                stacked + [*held[at], loc],
                [],
                work,
                flops=flops,
                name="advance",
            )
    (state,) = call(
        finish,
        [tall],
        spread(g) + [*held[3], loc],
        [info],
        [pltpu.VMEM(s, d) for s, d in blocks] + work + [pltpu.VMEM((80, 512), F32)],
        flops=flops,
        name="finish",
    )
    return state


def solution(mesh):
    fine = Mesh(mesh.devices.reshape(8, 4, 4, 2), ("z", "y", "x", "c"))
    tiles = ("y", "x", "c")
    in_specs = (P("z", tiles), P(), P(), P(), P(), P(tiles + ("z",), None))
    out_specs = P(None, tiles + ("z",))
    return jax.shard_map(per_device, mesh=fine, in_specs=in_specs, out_specs=out_specs, check_vma=False)
```

```python
import jax
import jax.numpy as jnp
from jax import lax
from jax.experimental import pallas as pl
from jax.experimental.pallas import tpu as pltpu
from jax.sharding import Mesh, PartitionSpec as P

EPS = 1e-05
LOC_TABLE = (1.0, 0.6848958, 0.2083333, 0.0164931, 0.0)
F32 = jnp.float32
BF16 = jnp.bfloat16
VMEM = pl.BlockSpec(memory_space=pltpu.VMEM)
SMEM = pl.BlockSpec(memory_space=pltpu.SMEM)

CHUNK = 168
PACK = 192


def call(body, shapes, args, scalars, scratch=(), flops=0, name=None):
    outs = [jax.ShapeDtypeStruct(s, d) for s, d in shapes]
    moved = sum(a.size * a.dtype.itemsize for a in args) + sum(o.size * o.dtype.itemsize for o in outs)
    made = pl.pallas_call(
        body,
        out_shape=outs,
        in_specs=[SMEM] * len(scalars) + [VMEM] * len(args),
        out_specs=[VMEM] * len(outs),
        scratch_shapes=list(scratch),
        compiler_params=pltpu.CompilerParams(vmem_limit_bytes=40 * 2**20),
        cost_estimate=pl.CostEstimate(flops=flops, bytes_accessed=moved, transcendentals=0),
        name=name,
    )(*scalars, *args)
    return list(made)


def lanes(info_ref):
    return pl.ds(pl.multiple_of(info_ref[1] * 128, 128), 128)


def pick(info_ref, first_by, core, index_ref, ext_ref, tile, start_ref, out_refs):
    first = info_ref[0]

    def group(n, carry):
        by = first_by ^ n
        block = (info_ref[3] ^ by) * 2 + core
        here = pl.ds(pl.multiple_of(block * 128, 128), 128)
        for k in range(4):
            local = [index_ref[b, k : k + 1, here] - first for b in range(4)]
            tail = jnp.concatenate([jnp.broadcast_to(v, (2, 128)) for v in local], axis=0)
            wide = [jnp.broadcast_to(v, (8, 128)) for v in local] + [tail]
            for b in range(5):
                low = wide[b] & 127
                high = wide[b] >> 7
                top = 0 if b < 4 else 8
                rows = slice(40 * k + 8 * b, 40 * k + 8 * b + 8)
                acc = jnp.zeros((8, 128), F32) if start_ref is None else start_ref[by, rows, :]
                for part in range(32):
                    source = ext_ref[top : top + 8, part * 128 : (part + 1) * 128]
                    got = jnp.take_along_axis(source, low, axis=1)
                    acc = jnp.where(high == part, got, acc)
                out_refs[n, rows, :] = acc
        rest = tile if start_ref is None else tile + start_ref[by, 160:168, :]
        out_refs[n, 160:168, :] = rest
        return carry

    lax.fori_loop(0, out_refs.shape[0], group, 0)


def collect_other(info_ref, index_ref, ens_ref, class_ref, out_ref, ext_ref, tile_ref, row_ref):
    ext_ref[0:8, :] = ens_ref[0:8, :]
    for r in range(4):
        ext_ref[8 + 2 * r : 10 + 2 * r, :] = ens_ref[8:10, :]
    even = lax.broadcasted_iota(jnp.int32, (32, 16), 0) == 2 * lax.broadcasted_iota(jnp.int32, (32, 16), 1)
    odd = lax.broadcasted_iota(jnp.int32, (32, 16), 0) == 2 * lax.broadcasted_iota(jnp.int32, (32, 16), 1) + 1
    mix = jnp.where(even, 1.0, jnp.where(odd, 8.0, 0.0)).astype(BF16)
    pairs = jnp.dot(class_ref[...].astype(F32).astype(BF16), mix, preferred_element_type=F32)
    for half in range(2):
        for i in range(4):
            row_ref[0:1, 64 * half + 16 * i : 64 * half + 16 * i + 16] = pairs[i : i + 1, :]
    row = lax.broadcasted_iota(jnp.int32, (8, 128), 0) == (info_ref[2] & 1) * 4 + info_ref[3]
    lane = (lax.broadcasted_iota(jnp.int32, (8, 128), 1) >> 6) == info_ref[4]
    tile = jnp.where(row & lane, jnp.broadcast_to(row_ref[...], (8, 128)), 0.0)
    tile_ref[...] = tile
    pick(info_ref, 0, 1 - info_ref[4], index_ref, ext_ref, tile, None, out_ref)


def collect_own(info_ref, index_ref, ext_ref, tile_ref, out_ref):
    pick(info_ref, 2, info_ref[4], index_ref, ext_ref, tile_ref[...], None, out_ref)


def collect_rest(info_ref, index_ref, ext_ref, tile_ref, start_ref, p0_ref, p1_ref, work_ref):
    pick(info_ref, 1, info_ref[4], index_ref, ext_ref, tile_ref[...], start_ref, work_ref)
    p1_ref[...] = work_ref[0]
    p0_ref[...] = work_ref[1]


def add_cores(own_ref, other_ref, p2_ref, p3_ref):
    p2_ref[...] = own_ref[0] + other_ref[2]
    p3_ref[...] = own_ref[1] + other_ref[3]


def add_columns(p0_ref, p1_ref, p2_ref, p3_ref, out_ref):
    out_ref[...] = (p0_ref[...] + p1_ref[...]) + (p2_ref[...] + p3_ref[...])


def add_rows(info_ref, weight_ref, ext_ref, p0_ref, p1_ref, p2_ref, p3_ref, out_ref, sum_ref):
    parts = [p0_ref, p1_ref, p2_ref, p3_ref]
    sum_ref[...] = (p0_ref[0:160, :] + p1_ref[0:160, :]) + (p2_ref[0:160, :] + p3_ref[0:160, :])
    here = lanes(info_ref)
    head = jnp.zeros((8, 128), F32)
    tail = jnp.zeros((2, 128), F32)
    for k in range(4):
        weight = weight_ref[0, k : k + 1, here]
        head = head + sum_ref[40 * k : 40 * k + 8, :] * weight
        tail = tail + sum_ref[40 * k + 32 : 40 * k + 34, :] * weight
    classes = [jnp.zeros((8, 128), F32)] * 2
    for s in range(4):
        upper = (info_ref[2] ^ s) >> 1
        for t in range(2):
            classes[t] = classes[t] + jnp.where(upper == t, parts[s][160:168, :], 0.0)
    pair = lax.broadcasted_iota(jnp.int32, (8, 128), 0) >> 1
    for z in range(8):
        for k in range(4):
            out_ref[z, 24 * k : 24 * k + 24, :] = sum_ref[40 * k + 8 : 40 * k + 32, :]
            out_ref[z, 104 + 6 * k : 110 + 6 * k, :] = sum_ref[40 * k + 34 : 40 * k + 40, :]
        out_ref[z, 96:104, :] = head
        out_ref[z, 128:136, :] = jnp.zeros((8, 128), F32)
        out_ref[z, 128:130, :] = tail
        last = jnp.zeros((8, 128), F32)
        for i in range(4):
            at = slice(512 * z + 128 * i, 512 * z + 128 * i + 128)
            out_ref[z, 136 + 8 * i : 144 + 8 * i, :] = ext_ref[0:8, at]
            last = jnp.where(pair == i, ext_ref[8:16, at], last)
        out_ref[z, 168:176, :] = last
        for t in range(2):
            out_ref[z, 176 + 8 * t : 184 + 8 * t, :] = classes[t]


def increments(prior, value, errvar, out_ref, wide_ref):
    mean = jnp.mean(prior, axis=0, keepdims=True)
    anom = prior - mean
    var = jnp.sum(anom * anom, axis=0, keepdims=True) / 79.0
    inverse = 1.0 / (var + EPS)
    post_var = 1.0 / (inverse + 1.0 / errvar)
    post_mean = post_var * (mean * inverse + value / errvar)
    shrink = jnp.sqrt(errvar / (errvar + var))
    incr = post_mean - mean + (shrink - 1.0) * anom
    rest = inverse / 79.0
    wide_ref[0:80, :] = anom.astype(BF16).astype(F32)
    wide_ref[80:128, :] = jnp.zeros((48, 128), F32)
    for row in (80, 81, 82):
        part = rest.astype(BF16).astype(F32)
        wide_ref[row : row + 1, :] = part
        rest = rest - part
    out_ref[0:128, :] = jnp.transpose(wide_ref[...]).astype(BF16)
    out_ref[128:208, :] = incr.astype(BF16)


def first_batch(info_ref, pack_ref, value_ref, errvar_ref, out_ref, prior_ref, wide_ref):
    for z in range(8):
        prior_ref[8 * z : 8 * z + 8, :] = pack_ref[z, 96:104, :]
        prior_ref[64 + 2 * z : 66 + 2 * z, :] = pack_ref[z, 128:130, :]
    here = lanes(info_ref)
    increments(prior_ref[...], value_ref[0:1, here], errvar_ref[0:1, here], out_ref, wide_ref)


def center(x, out_ref):
    out_ref[0:80, :] = (x - jnp.mean(x, axis=0, keepdims=True)).astype(BF16)
    out_ref[80:128, :] = jnp.zeros((48, x.shape[1]), BF16)


def unpack(info_ref, pack_ref, index_ref, *refs):
    outs, centered, loc_ref = refs[:4], refs[4:8], refs[8]
    here = lanes(info_ref)
    table = pack_ref[:, 176:192, :].reshape(128, 128).astype(BF16)
    for b in range(4):
        for k in range(4):
            at = slice(128 * k, 128 * k + 128)
            for z in range(8):
                if b < 3:
                    outs[b][8 * z : 8 * z + 8, at] = pack_ref[z, 24 * k + 8 * b : 24 * k + 8 * b + 8, :]
                    outs[b][64 + 2 * z : 66 + 2 * z, at] = pack_ref[z, 104 + 6 * k + 2 * b : 106 + 6 * k + 2 * b, :]
                else:
                    outs[b][8 * z : 8 * z + 8, at] = pack_ref[z, 136 + 8 * k : 144 + 8 * k, :]
                    outs[b][64 + 2 * z : 66 + 2 * z, at] = pack_ref[z, 168 + 2 * k : 170 + 2 * k, :]
            if b < 3:
                block = index_ref[b + 1, k : k + 1, here] >> 7
            else:
                block = jnp.full((1, 128), info_ref[5] + k, jnp.int32)
            holder = ((block >> 2) & 7) * 16 + (block >> 6)
            own = (lax.broadcasted_iota(jnp.int32, (128, 128), 0) == holder).astype(F32).astype(BF16)
            found = lax.dot_general(table, own, (((0,), (0,)), ((), ())), preferred_element_type=F32)
            which = ((block >> 5) & 1) * 4 + (block & 3)
            pairs = jnp.zeros((16, 128), F32)
            for i in range(8):
                pairs = pairs + jnp.where(which == i, found[16 * i : 16 * i + 16, :], 0.0)
            odd = jnp.floor(pairs * 0.125)
            for top, level in ((0, pairs - 8.0 * odd), (16, odd)):
                weights = jnp.zeros((16, 128), F32)
                for n, w in enumerate(LOC_TABLE):
                    weights = weights + jnp.where(level == n, w, 0.0)
                loc_ref[b, top : top + 16, at] = weights
    for x_ref, c_ref in zip(outs, centered):
        center(x_ref[...], c_ref)


def slots(info_ref):
    here, core = info_ref[3], info_ref[4]
    straight = [(here ^ s) * 2 + core for s in range(4)]
    return straight + [(here ^ s) * 2 + 1 - core for s in range(4)]


def stack(info_ref, refs, anom_ref, incr_ref, inverse_ref):
    for slot, ref in zip(slots(info_ref), refs):
        at = pl.ds(pl.multiple_of(slot * 128, 128), 128)
        anom_ref[at, :] = ref[0:128, :]
        incr_ref[:, at] = ref[128:208, :]
    lane = lax.broadcasted_iota(jnp.int32, (128, 128), 0)
    parts = jnp.where((lane >= 80) & (lane < 83), 1.0, 0.0).astype(BF16)
    inverse_ref[...] = jnp.dot(anom_ref[...], parts, preferred_element_type=F32)


def moved(x_ref, centered_ref, loc_ref, at, batch, anom_ref, incr_ref, inverse_ref, cov_ref, gain_ref):
    cov_ref[...] = jnp.dot(anom_ref[...], centered_ref[...], preferred_element_type=F32)
    for ob in range(8):
        row = 16 * (ob % 2) + 4 * batch + ob // 2
        rows = slice(128 * ob, 128 * ob + 128)
        for k in range(4):
            cols = slice(128 * k, 128 * k + 128)
            gain = (cov_ref[rows, cols] * inverse_ref[rows, :]) * loc_ref[at, row : row + 1, cols]
            gain_ref[rows, cols] = gain.astype(BF16)
    return x_ref[...] + jnp.dot(incr_ref[...], gain_ref[...], preferred_element_type=F32)


def next_batch(batch):
    def body(info_ref, *refs):
        x_ref, c_ref, loc_ref, weight_ref, value_ref, errvar_ref = refs[8:14]
        out_ref, anom_ref, incr_ref, inverse_ref, cov_ref, gain_ref, wide_ref = refs[14:]
        stack(info_ref, refs[:8], anom_ref, incr_ref, inverse_ref)
        x = moved(x_ref, c_ref, loc_ref, batch - 1, batch - 1, anom_ref, incr_ref, inverse_ref, cov_ref, gain_ref)
        here = lanes(info_ref)
        prior = x[:, 0:128] * weight_ref[batch, 0:1, here]
        for k in range(1, 4):
            prior = prior + x[:, 128 * k : 128 * k + 128] * weight_ref[batch, k : k + 1, here]
        increments(prior, value_ref[batch : batch + 1, here], errvar_ref[batch : batch + 1, here], out_ref, wide_ref)

    return body


def advance(at, batch):
    def body(anom_ref, incr_ref, inverse_ref, x_ref, c_ref, loc_ref, out_ref, c_out_ref, cov_ref, gain_ref):
        x = moved(x_ref, c_ref, loc_ref, at, batch, anom_ref, incr_ref, inverse_ref, cov_ref, gain_ref)
        out_ref[...] = x
        center(x, c_out_ref)

    return body


def finish(info_ref, *refs):
    x_ref, c_ref, loc_ref, out_ref, anom_ref, incr_ref, inverse_ref, cov_ref, gain_ref, work_ref = refs[8:]
    stack(info_ref, refs[:8], anom_ref, incr_ref, inverse_ref)
    work_ref[...] = moved(x_ref, c_ref, loc_ref, 3, 3, anom_ref, incr_ref, inverse_ref, cov_ref, gain_ref)
    for z in range(8):
        out_ref[10 * z : 10 * z + 8, :] = work_ref[8 * z : 8 * z + 8, :]
        out_ref[10 * z + 8 : 10 * z + 10, :] = work_ref[64 + 2 * z : 66 + 2 * z, :]


def swap(a, axis, by, size):
    return lax.ppermute(a, axis, [(i, i ^ by) for i in range(size)])


def swaps(a, axis):
    got = {s: swap(a, axis, s, 4) for s in (1, 3, 2)}
    return [a, got[1], got[2], got[3]]


def spread(g, beside=()):
    own = swaps(g, "x")
    if beside:
        own[2], *beside = lax.optimization_barrier((own[2], *beside))
    return own + [swap(v, "c", 1, 2) for v in own], list(beside)


def per_device(ensemble, obs_index, obs_weight, obs_value, obs_error_var, loc_class):
    z, y, x, c = [lax.axis_index(n) for n in ("z", "y", "x", "c")]
    block = x * 2 + c
    info = jnp.stack([(y * 8 + block) * 4096, block, y, x, c, (y * 8 + block) * 32 + z * 4]).astype(jnp.int32)

    rows = [((CHUNK, 128), F32)]
    other, ext, tile = call(
        collect_other,
        [((4, CHUNK, 128), F32), ((16, 4096), F32), ((8, 128), F32)],
        [obs_index, ensemble, loc_class],
        [info],
        [pltpu.VMEM((1, 128), F32)],
        name="collect_other",
    )
    other = swap(other, "c", 1, 2)
    (own,) = call(collect_own, [((2, CHUNK, 128), F32)], [obs_index, ext, tile], [info], flops=10**9, name="collect_own")
    p2, p3 = call(add_cores, rows * 2, [own, other], [], name="add_cores")
    p2, p3 = swap(p2, "x", 2, 4), swap(p3, "x", 3, 4)
    p0, p1 = call(
        collect_rest,
        rows * 2,
        [obs_index, ext, tile, other],
        [info],
        [pltpu.VMEM((2, CHUNK, 128), F32)],
        flops=10**9,
        name="collect_rest",
    )
    sums = [p0, swap(p1, "x", 1, 4), p2, p3]
    (part,) = call(add_columns, rows, sums, [], name="add_columns")
    parts = swaps(part, "y")
    (pack,) = call(
        add_rows,
        [((8, PACK, 128), F32)],
        [obs_weight, ext] + parts,
        [info],
        [pltpu.VMEM((160, 128), F32)],
        name="add_rows",
    )
    pack = lax.all_to_all(pack, "z", 0, 0, tiled=True)

    tall, centered, sent = ((80, 512), F32), ((128, 512), BF16), ((208, 128), BF16)
    blocks = [((1024, 128), BF16), ((80, 1024), BF16), ((1024, 128), F32)]
    wide = pltpu.VMEM((128, 128), F32)
    work = [pltpu.VMEM((1024, 512), F32), pltpu.VMEM((1024, 512), BF16)]
    flops = 2 * 2 * 1024 * 128 * 512
    (g,) = call(
        first_batch,
        [sent],
        [pack, obs_value, obs_error_var],
        [info],
        [pltpu.VMEM((80, 128), F32), wide],
        name="first_batch",
    )
    *both, loc = call(
        unpack,
        [tall] * 4 + [centered] * 4 + [((4, 32, 512), F32)],
        [pack, obs_index],
        [info],
        flops=2 * 128 * 128 * 2048,
        name="unpack",
    )
    held = dict(enumerate(zip(both[:4], both[4:])))
    waiting = {}
    for batch in range(4):
        soon = sorted(waiting)[:2]
        beside = [a for at in soon for a in waiting[at]]
        got, beside = spread(g, beside)
        for n, at in enumerate(soon):
            waiting[at] = beside[2 * n : 2 * n + 2]
        held.update(waiting)
        if batch == 3:
            break
        g, *stacked = call(
            next_batch(batch + 1),
            [sent] + blocks,
            got + [*held[batch], loc, obs_weight, obs_value, obs_error_var],
            [info],
            work + [wide],
            flops=flops,
            name="next_batch",
        )
        waiting = {
            at: call(
                advance(at, batch),
                [tall, centered],
                stacked + [*held[at], loc],
                [],
                work,
                flops=flops,
                name="advance",
            )
            for at in range(batch + 1, 4)
        }
    (state,) = call(
        finish,
        [tall],
        got + [*held[3], loc],
        [info],
        [pltpu.VMEM(s, d) for s, d in blocks] + work + [pltpu.VMEM((80, 512), F32)],
        flops=flops,
        name="finish",
    )
    return state


def solution(mesh):
    fine = Mesh(mesh.devices.reshape(8, 4, 4, 2), ("z", "y", "x", "c"))
    tiles = ("y", "x", "c")
    in_specs = (P("z", tiles), P(), P(), P(), P(), P(tiles + ("z",), None))
    out_specs = P(None, tiles + ("z",))
    return jax.shard_map(per_device, mesh=fine, in_specs=in_specs, out_specs=out_specs, check_vma=False)
```

```python
import jax
import jax.numpy as jnp
from jax import lax
from jax.experimental import pallas as pl
from jax.experimental.pallas import tpu as pltpu
from jax.sharding import Mesh, PartitionSpec as P

EPS = 1e-05
LOC_TABLE = (1.0, 0.6848958, 0.2083333, 0.0164931, 0.0)
F32 = jnp.float32
BF16 = jnp.bfloat16
VMEM = pl.BlockSpec(memory_space=pltpu.VMEM)

CHUNK = 168
PACK = 192


def place():
    z, y, x, c = [lax.axis_index(n) for n in ("z", "y", "x", "c")]
    block = x * 2 + c
    return [(y * 8 + block) * 4096, block, y, x, c, (y * 8 + block) * 32 + z * 4]


def call(body, shapes, args, placed=True, scratch=(), flops=0, name=None):
    outs = [jax.ShapeDtypeStruct(s, d) for s, d in shapes]
    moved = sum(a.size * a.dtype.itemsize for a in args) + sum(o.size * o.dtype.itemsize for o in outs)
    made = pl.pallas_call(
        (lambda *refs: body(place(), *refs)) if placed else body,
        out_shape=outs,
        in_specs=[VMEM] * len(args),
        out_specs=[VMEM] * len(outs),
        scratch_shapes=list(scratch),
        compiler_params=pltpu.CompilerParams(vmem_limit_bytes=16 * 2**20),
        cost_estimate=pl.CostEstimate(flops=flops, bytes_accessed=moved, transcendentals=0),
        name=name,
    )(*args)
    return list(made)


def lanes(info):
    return pl.ds(pl.multiple_of(info[1] * 128, 128), 128)


def pick(info, first_by, core, index_ref, ext_ref, tile, start_ref, out_refs):
    first = info[0]

    def group(n, carry):
        by = first_by ^ n
        block = (info[3] ^ by) * 2 + core
        here = pl.ds(pl.multiple_of(block * 128, 128), 128)
        for k in range(4):
            local = [index_ref[b, k : k + 1, here] - first for b in range(4)]
            tail = jnp.concatenate([jnp.broadcast_to(v, (2, 128)) for v in local], axis=0)
            wide = [jnp.broadcast_to(v, (8, 128)) for v in local] + [tail]
            for b in range(5):
                low = wide[b] & 127
                high = wide[b] >> 7
                top = 0 if b < 4 else 8
                rows = slice(40 * k + 8 * b, 40 * k + 8 * b + 8)
                acc = jnp.zeros((8, 128), F32) if start_ref is None else start_ref[by, rows, :]
                for part in range(32):
                    source = ext_ref[top : top + 8, part * 128 : (part + 1) * 128]
                    got = jnp.take_along_axis(source, low, axis=1)
                    acc = jnp.where(high == part, got, acc)
                out_refs[n, rows, :] = acc
        rest = tile if start_ref is None else tile + start_ref[by, 160:168, :]
        out_refs[n, 160:168, :] = rest
        return carry

    lax.fori_loop(0, out_refs.shape[0], group, 0)


def collect_other(info, index_ref, ens_ref, class_ref, out_ref, ext_ref, tile_ref, row_ref):
    ext_ref[0:8, :] = ens_ref[0:8, :]
    for r in range(4):
        ext_ref[8 + 2 * r : 10 + 2 * r, :] = ens_ref[8:10, :]
    even = lax.broadcasted_iota(jnp.int32, (32, 16), 0) == 2 * lax.broadcasted_iota(jnp.int32, (32, 16), 1)
    odd = lax.broadcasted_iota(jnp.int32, (32, 16), 0) == 2 * lax.broadcasted_iota(jnp.int32, (32, 16), 1) + 1
    mix = jnp.where(even, 1.0, jnp.where(odd, 8.0, 0.0)).astype(BF16)
    pairs = jnp.dot(class_ref[...].astype(F32).astype(BF16), mix, preferred_element_type=F32)
    for half in range(2):
        for i in range(4):
            row_ref[0:1, 64 * half + 16 * i : 64 * half + 16 * i + 16] = pairs[i : i + 1, :]
    row = lax.broadcasted_iota(jnp.int32, (8, 128), 0) == (info[2] & 1) * 4 + info[3]
    lane = (lax.broadcasted_iota(jnp.int32, (8, 128), 1) >> 6) == info[4]
    tile = jnp.where(row & lane, jnp.broadcast_to(row_ref[...], (8, 128)), 0.0)
    tile_ref[...] = tile
    pick(info, 0, 1 - info[4], index_ref, ext_ref, tile, None, out_ref)


def collect_own(info, index_ref, ext_ref, tile_ref, out_ref):
    pick(info, 2, info[4], index_ref, ext_ref, tile_ref[...], None, out_ref)


def collect_rest(info, index_ref, ext_ref, tile_ref, start_ref, p0_ref, p1_ref, work_ref):
    pick(info, 1, info[4], index_ref, ext_ref, tile_ref[...], start_ref, work_ref)
    p1_ref[...] = work_ref[0]
    p0_ref[...] = work_ref[1]


def add_cores(own_ref, other_ref, p2_ref, p3_ref):
    p2_ref[...] = own_ref[0] + other_ref[2]
    p3_ref[...] = own_ref[1] + other_ref[3]


def add_columns(p0_ref, p1_ref, p2_ref, p3_ref, out_ref):
    out_ref[...] = (p0_ref[...] + p1_ref[...]) + (p2_ref[...] + p3_ref[...])


def add_rows(info, weight_ref, ext_ref, p0_ref, p1_ref, p2_ref, p3_ref, out_ref, sum_ref):
    parts = [p0_ref, p1_ref, p2_ref, p3_ref]
    sum_ref[...] = (p0_ref[0:160, :] + p1_ref[0:160, :]) + (p2_ref[0:160, :] + p3_ref[0:160, :])
    here = lanes(info)
    head = jnp.zeros((8, 128), F32)
    tail = jnp.zeros((2, 128), F32)
    for k in range(4):
        weight = weight_ref[0, k : k + 1, here]
        head = head + sum_ref[40 * k : 40 * k + 8, :] * weight
        tail = tail + sum_ref[40 * k + 32 : 40 * k + 34, :] * weight
    classes = [jnp.zeros((8, 128), F32)] * 2
    for s in range(4):
        upper = (info[2] ^ s) >> 1
        for t in range(2):
            classes[t] = classes[t] + jnp.where(upper == t, parts[s][160:168, :], 0.0)
    pair = lax.broadcasted_iota(jnp.int32, (8, 128), 0) >> 1
    for z in range(8):
        for k in range(4):
            out_ref[z, 24 * k : 24 * k + 24, :] = sum_ref[40 * k + 8 : 40 * k + 32, :]
            out_ref[z, 104 + 6 * k : 110 + 6 * k, :] = sum_ref[40 * k + 34 : 40 * k + 40, :]
        out_ref[z, 96:104, :] = head
        out_ref[z, 128:136, :] = jnp.zeros((8, 128), F32)
        out_ref[z, 128:130, :] = tail
        last = jnp.zeros((8, 128), F32)
        for i in range(4):
            at = slice(512 * z + 128 * i, 512 * z + 128 * i + 128)
            out_ref[z, 136 + 8 * i : 144 + 8 * i, :] = ext_ref[0:8, at]
            last = jnp.where(pair == i, ext_ref[8:16, at], last)
        out_ref[z, 168:176, :] = last
        for t in range(2):
            out_ref[z, 176 + 8 * t : 184 + 8 * t, :] = classes[t]


def increments(prior, value, errvar, out_ref, wide_ref):
    mean = jnp.mean(prior, axis=0, keepdims=True)
    anom = prior - mean
    var = jnp.sum(anom * anom, axis=0, keepdims=True) / 79.0
    inverse = 1.0 / (var + EPS)
    post_var = 1.0 / (inverse + 1.0 / errvar)
    post_mean = post_var * (mean * inverse + value / errvar)
    shrink = jnp.sqrt(errvar / (errvar + var))
    incr = post_mean - mean + (shrink - 1.0) * anom
    rest = inverse / 79.0
    wide_ref[0:80, :] = anom.astype(BF16).astype(F32)
    wide_ref[80:128, :] = jnp.zeros((48, 128), F32)
    for row in (80, 81, 82):
        part = rest.astype(BF16).astype(F32)
        wide_ref[row : row + 1, :] = part
        rest = rest - part
    out_ref[0:128, :] = jnp.transpose(wide_ref[...]).astype(BF16)
    out_ref[128:208, :] = incr.astype(BF16)


def first_batch(info, pack_ref, value_ref, errvar_ref, out_ref, prior_ref, wide_ref):
    for z in range(8):
        prior_ref[8 * z : 8 * z + 8, :] = pack_ref[z, 96:104, :]
        prior_ref[64 + 2 * z : 66 + 2 * z, :] = pack_ref[z, 128:130, :]
    here = lanes(info)
    increments(prior_ref[...], value_ref[0:1, here], errvar_ref[0:1, here], out_ref, wide_ref)


def center(x, out_ref):
    out_ref[0:80, :] = (x - jnp.mean(x, axis=0, keepdims=True)).astype(BF16)
    out_ref[80:128, :] = jnp.zeros((48, x.shape[1]), BF16)


def unpack(info, pack_ref, index_ref, *refs):
    outs, centered, loc_ref = refs[:4], refs[4:8], refs[8]
    here = lanes(info)
    table = pack_ref[:, 176:192, :].reshape(128, 128).astype(BF16)
    for b in range(4):
        for k in range(4):
            at = slice(128 * k, 128 * k + 128)
            for z in range(8):
                if b < 3:
                    outs[b][8 * z : 8 * z + 8, at] = pack_ref[z, 24 * k + 8 * b : 24 * k + 8 * b + 8, :]
                    outs[b][64 + 2 * z : 66 + 2 * z, at] = pack_ref[z, 104 + 6 * k + 2 * b : 106 + 6 * k + 2 * b, :]
                else:
                    outs[b][8 * z : 8 * z + 8, at] = pack_ref[z, 136 + 8 * k : 144 + 8 * k, :]
                    outs[b][64 + 2 * z : 66 + 2 * z, at] = pack_ref[z, 168 + 2 * k : 170 + 2 * k, :]
            if b < 3:
                block = index_ref[b + 1, k : k + 1, here] >> 7
            else:
                block = jnp.full((1, 128), info[5] + k, jnp.int32)
            holder = ((block >> 2) & 7) * 16 + (block >> 6)
            own = (lax.broadcasted_iota(jnp.int32, (128, 128), 0) == holder).astype(F32).astype(BF16)
            found = lax.dot_general(table, own, (((0,), (0,)), ((), ())), preferred_element_type=F32)
            which = ((block >> 5) & 1) * 4 + (block & 3)
            pairs = jnp.zeros((16, 128), F32)
            for i in range(8):
                pairs = pairs + jnp.where(which == i, found[16 * i : 16 * i + 16, :], 0.0)
            odd = jnp.floor(pairs * 0.125)
            for core, level in ((info[4], pairs - 8.0 * odd), (1 - info[4], odd)):
                weights = jnp.zeros((16, 128), F32)
                for n, w in enumerate(LOC_TABLE):
                    weights = weights + jnp.where(level == n, w, 0.0)
                loc_ref[b, pl.ds(pl.multiple_of(core * 16, 16), 16), at] = weights
    for x_ref, c_ref in zip(outs, centered):
        center(x_ref[...], c_ref)


def stack(info, refs, anom_ref, incr_ref, inverse_ref):
    for s, ref in enumerate(refs):
        at = pl.ds(pl.multiple_of((info[3] ^ s) * 128, 128), 128)
        anom_ref[at, :] = ref[0:128, :]
        incr_ref[:, at] = ref[128:208, :]
    lane = lax.broadcasted_iota(jnp.int32, (128, 128), 0)
    parts = jnp.where((lane >= 80) & (lane < 83), 1.0, 0.0).astype(BF16)
    inverse_ref[...] = jnp.dot(anom_ref[...], parts, preferred_element_type=F32)


def change(other, centered_ref, loc_ref, at, batch, anom_ref, incr_ref, inverse_ref, cov_ref, gain_ref):
    cov_ref[...] = jnp.dot(anom_ref[...], centered_ref[...], preferred_element_type=F32)
    for p in range(4):
        row = 16 * other + 4 * batch + p
        rows = slice(128 * p, 128 * p + 128)
        for k in range(4):
            cols = slice(128 * k, 128 * k + 128)
            gain_ref[rows, cols] = ((cov_ref[rows, cols] * inverse_ref[rows, :]) * loc_ref[at, row : row + 1, cols]).astype(BF16)
    return jnp.dot(incr_ref[...], gain_ref[...], preferred_element_type=F32)


def half(at, batch):
    def body(info, *refs):
        c_ref, loc_ref, part_ref, anom_ref, incr_ref, inverse_ref, cov_ref, gain_ref = refs[4:]
        stack(info, refs[:4], anom_ref, incr_ref, inverse_ref)
        part_ref[...] = change(0, c_ref, loc_ref, at, batch, anom_ref, incr_ref, inverse_ref, cov_ref, gain_ref)

    return body


def next_batch(batch):
    def body(info, *refs):
        x_ref, c_ref, loc_ref, part_ref, weight_ref, value_ref, errvar_ref = refs[4:11]
        out_ref, anom_ref, incr_ref, inverse_ref, cov_ref, gain_ref, wide_ref = refs[11:]
        stack(info, refs[:4], anom_ref, incr_ref, inverse_ref)
        blocks = (anom_ref, incr_ref, inverse_ref, cov_ref, gain_ref)
        x = x_ref[...] + (part_ref[...] + change(1, c_ref, loc_ref, batch - 1, batch - 1, *blocks))
        here = lanes(info)
        prior = x[:, 0:128] * weight_ref[batch, 0:1, here]
        for k in range(1, 4):
            prior = prior + x[:, 128 * k : 128 * k + 128] * weight_ref[batch, k : k + 1, here]
        increments(prior, value_ref[batch : batch + 1, here], errvar_ref[batch : batch + 1, here], out_ref, wide_ref)

    return body


def advance(at, batch):
    def body(*refs):
        own, other = refs[:3], refs[3:6]
        x_ref, c_ref, loc_ref, out_ref, c_out_ref, cov_ref, gain_ref = refs[6:]
        first = change(0, c_ref, loc_ref, at, batch, *own, cov_ref, gain_ref)
        x = x_ref[...] + (first + change(1, c_ref, loc_ref, at, batch, *other, cov_ref, gain_ref))
        out_ref[...] = x
        center(x, c_out_ref)

    return body


def finish(info, *refs):
    x_ref, c_ref, loc_ref, part_ref, out_ref, anom_ref, incr_ref, inverse_ref, cov_ref, gain_ref, work_ref = refs[4:]
    stack(info, refs[:4], anom_ref, incr_ref, inverse_ref)
    blocks = (anom_ref, incr_ref, inverse_ref, cov_ref, gain_ref)
    work_ref[...] = x_ref[...] + (part_ref[...] + change(1, c_ref, loc_ref, 3, 3, *blocks))
    for z in range(8):
        out_ref[10 * z : 10 * z + 8, :] = work_ref[8 * z : 8 * z + 8, :]
        out_ref[10 * z + 8 : 10 * z + 10, :] = work_ref[64 + 2 * z : 66 + 2 * z, :]


def swap(a, axis, by, size):
    return lax.ppermute(a, axis, [(i, i ^ by) for i in range(size)])


def swaps(a, axis):
    got = {s: swap(a, axis, s, 4) for s in (1, 3, 2)}
    return [a, got[1], got[2], got[3]]


def spread(g, beside=()):
    own = swaps(g, "x")
    if beside:
        own[2], *beside = lax.optimization_barrier((own[2], *beside))
    return own, [swap(v, "c", 1, 2) for v in own], list(beside)


def per_device(ensemble, obs_index, obs_weight, obs_value, obs_error_var, loc_class):
    rows = [((CHUNK, 128), F32)]
    other, ext, tile = call(
        collect_other,
        [((4, CHUNK, 128), F32), ((16, 4096), F32), ((8, 128), F32)],
        [obs_index, ensemble, loc_class],
        True,
        [pltpu.VMEM((1, 128), F32)],
        name="collect_other",
    )
    other = swap(other, "c", 1, 2)
    (own,) = call(collect_own, [((2, CHUNK, 128), F32)], [obs_index, ext, tile], True, flops=10**9, name="collect_own")
    p2, p3 = call(add_cores, rows * 2, [own, other], False, name="add_cores")
    p2, p3 = swap(p2, "x", 2, 4), swap(p3, "x", 3, 4)
    p0, p1 = call(
        collect_rest,
        rows * 2,
        [obs_index, ext, tile, other],
        True,
        [pltpu.VMEM((2, CHUNK, 128), F32)],
        flops=10**9,
        name="collect_rest",
    )
    sums = [p0, swap(p1, "x", 1, 4), p2, p3]
    (part,) = call(add_columns, rows, sums, False, name="add_columns")
    parts = swaps(part, "y")
    (pack,) = call(
        add_rows,
        [((8, PACK, 128), F32)],
        [obs_weight, ext] + parts,
        True,
        [pltpu.VMEM((160, 128), F32)],
        name="add_rows",
    )
    pack = lax.all_to_all(pack, "z", 0, 0, tiled=True)

    tall, centered, sent = ((80, 512), F32), ((128, 512), BF16), ((208, 128), BF16)
    blocks = [((512, 128), BF16), ((80, 512), BF16), ((512, 128), F32)]
    wide = pltpu.VMEM((128, 128), F32)
    work = [pltpu.VMEM((512, 512), F32), pltpu.VMEM((512, 512), BF16)]
    flops = 2 * 2 * 1024 * 128 * 512
    (g,) = call(
        first_batch,
        [sent],
        [pack, obs_value, obs_error_var],
        True,
        [pltpu.VMEM((80, 128), F32), wide],
        name="first_batch",
    )
    *both, loc = call(
        unpack,
        [tall] * 4 + [centered] * 4 + [((4, 32, 512), F32)],
        [pack, obs_index],
        True,
        flops=2 * 128 * 128 * 2048,
        name="unpack",
    )
    held = dict(enumerate(zip(both[:4], both[4:])))
    waiting = {}
    for batch in range(4):
        soon = sorted(waiting)[:2]
        own, other, beside = spread(g, [a for at in soon for a in waiting[at]])
        for n, at in enumerate(soon):
            waiting[at] = beside[2 * n : 2 * n + 2]
        held.update(waiting)
        at = min(batch, 3)
        part, *first = call(
            half(at, batch),
            [tall] + blocks * (batch < 3),
            own + [held[at][1], loc],
            True,
            work if batch < 3 else [pltpu.VMEM(s, d) for s, d in blocks] + work,
            flops=flops // 2,
            name="half",
        )
        if batch == 3:
            break
        g, *second = call(
            next_batch(batch + 1),
            [sent] + blocks,
            other + [*held[at], loc, part, obs_weight, obs_value, obs_error_var],
            True,
            work + [wide],
            flops=flops // 2,
            name="next_batch",
        )
        waiting = {
            at: call(
                advance(at, batch),
                [tall, centered],
                first + second + [*held[at], loc],
                False,
                work,
                flops=flops,
                name="advance",
            )
            for at in range(batch + 1, 4)
        }
    (state,) = call(
        finish,
        [tall],
        other + [*held[3], loc, part],
        True,
        [pltpu.VMEM(s, d) for s, d in blocks] + work + [pltpu.VMEM((80, 512), F32)],
        flops=flops // 2,
        name="finish",
    )
    return state


def solution(mesh):
    fine = Mesh(mesh.devices.reshape(8, 4, 4, 2), ("z", "y", "x", "c"))
    tiles = ("y", "x", "c")
    in_specs = (P("z", tiles), P(), P(), P(), P(), P(tiles + ("z",), None))
    out_specs = P(None, tiles + ("z",))
    return jax.shard_map(per_device, mesh=fine, in_specs=in_specs, out_specs=out_specs, check_vma=False)
```

```python
import jax
import jax.numpy as jnp
from jax import lax
from jax.experimental import pallas as pl
from jax.experimental.pallas import tpu as pltpu
from jax.sharding import Mesh, PartitionSpec as P

EPS = 1e-05
LOC_TABLE = (1.0, 0.6848958, 0.2083333, 0.0164931, 0.0)
F32 = jnp.float32
BF16 = jnp.bfloat16
VMEM = pl.BlockSpec(memory_space=pltpu.VMEM)

CHUNK = 168
PACK = 192


def place():
    z, y, x, c = [lax.axis_index(n) for n in ("z", "y", "x", "c")]
    block = x * 2 + c
    return [(y * 8 + block) * 4096, block, y, x, c, (y * 8 + block) * 32 + z * 4]


def call(body, shapes, args, placed=True, scratch=(), flops=0, name=None):
    outs = [jax.ShapeDtypeStruct(s, d) for s, d in shapes]
    moved = sum(a.size * a.dtype.itemsize for a in args) + sum(o.size * o.dtype.itemsize for o in outs)
    made = pl.pallas_call(
        (lambda *refs: body(place(), *refs)) if placed else body,
        out_shape=outs,
        in_specs=[VMEM] * len(args),
        out_specs=[VMEM] * len(outs),
        scratch_shapes=list(scratch),
        compiler_params=pltpu.CompilerParams(vmem_limit_bytes=16 * 2**20),
        cost_estimate=pl.CostEstimate(flops=flops, bytes_accessed=moved, transcendentals=0),
        name=name,
    )(*args)
    return list(made)


def lanes(info):
    return pl.ds(pl.multiple_of(info[1] * 128, 128), 128)


def pick(info, first_by, core, index_ref, ext_ref, tile, start_ref, out_refs):
    first = info[0]

    def group(n, carry):
        by = first_by ^ n
        block = (info[3] ^ by) * 2 + core
        here = pl.ds(pl.multiple_of(block * 128, 128), 128)
        for k in range(4):
            local = [index_ref[b, k : k + 1, here] - first for b in range(4)]
            tail = jnp.concatenate([jnp.broadcast_to(v, (2, 128)) for v in local], axis=0)
            wide = [jnp.broadcast_to(v, (8, 128)) for v in local] + [tail]
            for b in range(5):
                low = wide[b] & 127
                high = wide[b] >> 7
                top = 0 if b < 4 else 8
                rows = slice(40 * k + 8 * b, 40 * k + 8 * b + 8)
                acc = jnp.zeros((8, 128), F32) if start_ref is None else start_ref[by, rows, :]
                for part in range(32):
                    source = ext_ref[top : top + 8, part * 128 : (part + 1) * 128]
                    got = jnp.take_along_axis(source, low, axis=1)
                    acc = jnp.where(high == part, got, acc)
                out_refs[n, rows, :] = acc
        rest = tile if start_ref is None else tile + start_ref[by, 160:168, :]
        out_refs[n, 160:168, :] = rest
        return carry

    lax.fori_loop(0, out_refs.shape[0], group, 0)


def collect_other(info, index_ref, ens_ref, class_ref, out_ref, ext_ref, tile_ref, row_ref):
    ext_ref[0:8, :] = ens_ref[0:8, :]
    for r in range(4):
        ext_ref[8 + 2 * r : 10 + 2 * r, :] = ens_ref[8:10, :]
    even = lax.broadcasted_iota(jnp.int32, (32, 16), 0) == 2 * lax.broadcasted_iota(jnp.int32, (32, 16), 1)
    odd = lax.broadcasted_iota(jnp.int32, (32, 16), 0) == 2 * lax.broadcasted_iota(jnp.int32, (32, 16), 1) + 1
    mix = jnp.where(even, 1.0, jnp.where(odd, 8.0, 0.0)).astype(BF16)
    pairs = jnp.dot(class_ref[...].astype(F32).astype(BF16), mix, preferred_element_type=F32)
    for half in range(2):
        for i in range(4):
            row_ref[0:1, 64 * half + 16 * i : 64 * half + 16 * i + 16] = pairs[i : i + 1, :]
    row = lax.broadcasted_iota(jnp.int32, (8, 128), 0) == (info[2] & 1) * 4 + info[3]
    lane = (lax.broadcasted_iota(jnp.int32, (8, 128), 1) >> 6) == info[4]
    tile = jnp.where(row & lane, jnp.broadcast_to(row_ref[...], (8, 128)), 0.0)
    tile_ref[...] = tile
    pick(info, 0, 1 - info[4], index_ref, ext_ref, tile, None, out_ref)


def collect_own(info, index_ref, ext_ref, tile_ref, out_ref):
    pick(info, 2, info[4], index_ref, ext_ref, tile_ref[...], None, out_ref)


def collect_rest(info, index_ref, ext_ref, tile_ref, start_ref, p0_ref, p1_ref, work_ref):
    pick(info, 1, info[4], index_ref, ext_ref, tile_ref[...], start_ref, work_ref)
    p1_ref[...] = work_ref[0]
    p0_ref[...] = work_ref[1]


def add_cores(own_ref, other_ref, p2_ref, p3_ref):
    p2_ref[...] = own_ref[0] + other_ref[2]
    p3_ref[...] = own_ref[1] + other_ref[3]


def add_columns(info, weight_ref, p0_ref, p1_ref, p2_ref, p3_ref, out_ref, sum_ref):
    sum_ref[...] = (p0_ref[...] + p1_ref[...]) + (p2_ref[...] + p3_ref[...])
    here = lanes(info)
    head = jnp.zeros((8, 128), F32)
    tail = jnp.zeros((2, 128), F32)
    for k in range(4):
        weight = weight_ref[0, k : k + 1, here]
        head = head + sum_ref[40 * k : 40 * k + 8, :] * weight
        tail = tail + sum_ref[40 * k + 32 : 40 * k + 34, :] * weight
        out_ref[24 * k : 24 * k + 24, :] = sum_ref[40 * k + 8 : 40 * k + 32, :]
        out_ref[104 + 6 * k : 110 + 6 * k, :] = sum_ref[40 * k + 34 : 40 * k + 40, :]
    out_ref[96:104, :] = head
    out_ref[128:136, :] = jnp.zeros((8, 128), F32)
    out_ref[128:130, :] = tail
    out_ref[136:144, :] = sum_ref[160:168, :]


def add_rows(info, ext_ref, p0_ref, p1_ref, p2_ref, p3_ref, out_ref):
    parts = [p0_ref, p1_ref, p2_ref, p3_ref]
    total = (p0_ref[0:136, :] + p1_ref[0:136, :]) + (p2_ref[0:136, :] + p3_ref[0:136, :])
    classes = [jnp.zeros((8, 128), F32)] * 2
    for s in range(4):
        upper = (info[2] ^ s) >> 1
        for t in range(2):
            classes[t] = classes[t] + jnp.where(upper == t, parts[s][136:144, :], 0.0)
    pair = lax.broadcasted_iota(jnp.int32, (8, 128), 0) >> 1
    for z in range(8):
        out_ref[z, 0:136, :] = total
        last = jnp.zeros((8, 128), F32)
        for i in range(4):
            at = slice(512 * z + 128 * i, 512 * z + 128 * i + 128)
            out_ref[z, 136 + 8 * i : 144 + 8 * i, :] = ext_ref[0:8, at]
            last = jnp.where(pair == i, ext_ref[8:16, at], last)
        out_ref[z, 168:176, :] = last
        for t in range(2):
            out_ref[z, 176 + 8 * t : 184 + 8 * t, :] = classes[t]


def increments(prior, value, errvar, out_ref, wide_ref):
    mean = jnp.mean(prior, axis=0, keepdims=True)
    anom = prior - mean
    var = jnp.sum(anom * anom, axis=0, keepdims=True) / 79.0
    inverse = 1.0 / (var + EPS)
    post_var = 1.0 / (inverse + 1.0 / errvar)
    post_mean = post_var * (mean * inverse + value / errvar)
    shrink = jnp.sqrt(errvar / (errvar + var))
    incr = post_mean - mean + (shrink - 1.0) * anom
    rest = inverse / 79.0
    wide_ref[0:80, :] = anom.astype(BF16).astype(F32)
    wide_ref[80:128, :] = jnp.zeros((48, 128), F32)
    for row in (80, 81, 82):
        part = rest.astype(BF16).astype(F32)
        wide_ref[row : row + 1, :] = part
        rest = rest - part
    out_ref[0:128, :] = jnp.transpose(wide_ref[...]).astype(BF16)
    out_ref[128:208, :] = incr.astype(BF16)


def first_batch(info, pack_ref, value_ref, errvar_ref, out_ref, prior_ref, wide_ref):
    for z in range(8):
        prior_ref[8 * z : 8 * z + 8, :] = pack_ref[z, 96:104, :]
        prior_ref[64 + 2 * z : 66 + 2 * z, :] = pack_ref[z, 128:130, :]
    here = lanes(info)
    increments(prior_ref[...], value_ref[0:1, here], errvar_ref[0:1, here], out_ref, wide_ref)


def center(x, out_ref):
    out_ref[0:80, :] = (x - jnp.mean(x, axis=0, keepdims=True)).astype(BF16)
    out_ref[80:128, :] = jnp.zeros((48, x.shape[1]), BF16)


def unpack(info, pack_ref, index_ref, *refs):
    outs, centered, loc_ref = refs[:4], refs[4:8], refs[8]
    here = lanes(info)
    table = pack_ref[:, 176:192, :].reshape(128, 128).astype(BF16)
    for b in range(4):
        for k in range(4):
            at = slice(128 * k, 128 * k + 128)
            for z in range(8):
                if b < 3:
                    outs[b][8 * z : 8 * z + 8, at] = pack_ref[z, 24 * k + 8 * b : 24 * k + 8 * b + 8, :]
                    outs[b][64 + 2 * z : 66 + 2 * z, at] = pack_ref[z, 104 + 6 * k + 2 * b : 106 + 6 * k + 2 * b, :]
                else:
                    outs[b][8 * z : 8 * z + 8, at] = pack_ref[z, 136 + 8 * k : 144 + 8 * k, :]
                    outs[b][64 + 2 * z : 66 + 2 * z, at] = pack_ref[z, 168 + 2 * k : 170 + 2 * k, :]
            if b < 3:
                block = index_ref[b + 1, k : k + 1, here] >> 7
            else:
                block = jnp.full((1, 128), info[5] + k, jnp.int32)
            holder = ((block >> 2) & 7) * 16 + (block >> 6)
            own = (lax.broadcasted_iota(jnp.int32, (128, 128), 0) == holder).astype(F32).astype(BF16)
            found = lax.dot_general(table, own, (((0,), (0,)), ((), ())), preferred_element_type=F32)
            which = ((block >> 5) & 1) * 4 + (block & 3)
            pairs = jnp.zeros((16, 128), F32)
            for i in range(8):
                pairs = pairs + jnp.where(which == i, found[16 * i : 16 * i + 16, :], 0.0)
            odd = jnp.floor(pairs * 0.125)
            for core, level in ((info[4], pairs - 8.0 * odd), (1 - info[4], odd)):
                weights = jnp.zeros((16, 128), F32)
                for n, w in enumerate(LOC_TABLE):
                    weights = weights + jnp.where(level == n, w, 0.0)
                loc_ref[b, pl.ds(pl.multiple_of(core * 16, 16), 16), at] = weights
    for x_ref, c_ref in zip(outs, centered):
        center(x_ref[...], c_ref)


def stack(info, refs, anom_ref, incr_ref, inverse_ref):
    for s, ref in enumerate(refs):
        at = pl.ds(pl.multiple_of((info[3] ^ s) * 128, 128), 128)
        anom_ref[at, :] = ref[0:128, :]
        incr_ref[:, at] = ref[128:208, :]
    lane = lax.broadcasted_iota(jnp.int32, (128, 128), 0)
    parts = jnp.where((lane >= 80) & (lane < 83), 1.0, 0.0).astype(BF16)
    inverse_ref[...] = jnp.dot(anom_ref[...], parts, preferred_element_type=F32)


def change(other, centered_ref, loc_ref, at, batch, anom_ref, incr_ref, inverse_ref, cov_ref, gain_ref):
    cov_ref[...] = jnp.dot(anom_ref[...], centered_ref[...], preferred_element_type=F32)
    for p in range(4):
        row = 16 * other + 4 * batch + p
        rows = slice(128 * p, 128 * p + 128)
        for k in range(4):
            cols = slice(128 * k, 128 * k + 128)
            gain_ref[rows, cols] = ((cov_ref[rows, cols] * inverse_ref[rows, :]) * loc_ref[at, row : row + 1, cols]).astype(BF16)
    return jnp.dot(incr_ref[...], gain_ref[...], preferred_element_type=F32)


def half(at, batch):
    def body(info, *refs):
        c_ref, loc_ref, part_ref, anom_ref, incr_ref, inverse_ref, cov_ref, gain_ref = refs[4:]
        stack(info, refs[:4], anom_ref, incr_ref, inverse_ref)
        part_ref[...] = change(0, c_ref, loc_ref, at, batch, anom_ref, incr_ref, inverse_ref, cov_ref, gain_ref)

    return body


def next_batch(batch):
    def body(info, *refs):
        x_ref, c_ref, loc_ref, part_ref, weight_ref, value_ref, errvar_ref = refs[4:11]
        out_ref, anom_ref, incr_ref, inverse_ref, cov_ref, gain_ref, wide_ref = refs[11:]
        stack(info, refs[:4], anom_ref, incr_ref, inverse_ref)
        blocks = (anom_ref, incr_ref, inverse_ref, cov_ref, gain_ref)
        x = x_ref[...] + (part_ref[...] + change(1, c_ref, loc_ref, batch - 1, batch - 1, *blocks))
        here = lanes(info)
        prior = x[:, 0:128] * weight_ref[batch, 0:1, here]
        for k in range(1, 4):
            prior = prior + x[:, 128 * k : 128 * k + 128] * weight_ref[batch, k : k + 1, here]
        increments(prior, value_ref[batch : batch + 1, here], errvar_ref[batch : batch + 1, here], out_ref, wide_ref)

    return body


def advance(at, batch):
    def body(*refs):
        own, other = refs[:3], refs[3:6]
        x_ref, c_ref, loc_ref, out_ref, c_out_ref, cov_ref, gain_ref = refs[6:]
        first = change(0, c_ref, loc_ref, at, batch, *own, cov_ref, gain_ref)
        x = x_ref[...] + (first + change(1, c_ref, loc_ref, at, batch, *other, cov_ref, gain_ref))
        out_ref[...] = x
        center(x, c_out_ref)

    return body


def finish(info, *refs):
    x_ref, c_ref, loc_ref, part_ref, out_ref, anom_ref, incr_ref, inverse_ref, cov_ref, gain_ref, work_ref = refs[4:]
    stack(info, refs[:4], anom_ref, incr_ref, inverse_ref)
    blocks = (anom_ref, incr_ref, inverse_ref, cov_ref, gain_ref)
    work_ref[...] = x_ref[...] + (part_ref[...] + change(1, c_ref, loc_ref, 3, 3, *blocks))
    for z in range(8):
        out_ref[10 * z : 10 * z + 8, :] = work_ref[8 * z : 8 * z + 8, :]
        out_ref[10 * z + 8 : 10 * z + 10, :] = work_ref[64 + 2 * z : 66 + 2 * z, :]


def swap(a, axis, by, size):
    return lax.ppermute(a, axis, [(i, i ^ by) for i in range(size)])


def swaps(a, axis):
    got = {s: swap(a, axis, s, 4) for s in (1, 3, 2)}
    return [a, got[1], got[2], got[3]]


def spread(g, beside=()):
    own = swaps(g, "x")
    if beside:
        own[2], *beside = lax.optimization_barrier((own[2], *beside))
    return own, [swap(v, "c", 1, 2) for v in own], list(beside)


def per_device(ensemble, obs_index, obs_weight, obs_value, obs_error_var, loc_class):
    rows = [((CHUNK, 128), F32)]
    other, ext, tile = call(
        collect_other,
        [((4, CHUNK, 128), F32), ((16, 4096), F32), ((8, 128), F32)],
        [obs_index, ensemble, loc_class],
        True,
        [pltpu.VMEM((1, 128), F32)],
        name="collect_other",
    )
    other = swap(other, "c", 1, 2)
    (own,) = call(collect_own, [((2, CHUNK, 128), F32)], [obs_index, ext, tile], True, flops=10**9, name="collect_own")
    p2, p3 = call(add_cores, rows * 2, [own, other], False, name="add_cores")
    p2, p3 = swap(p2, "x", 2, 4), swap(p3, "x", 3, 4)
    p0, p1 = call(
        collect_rest,
        rows * 2,
        [obs_index, ext, tile, other],
        True,
        [pltpu.VMEM((2, CHUNK, 128), F32)],
        flops=10**9,
        name="collect_rest",
    )
    sums = [p0, swap(p1, "x", 1, 4), p2, p3]
    (part,) = call(
        add_columns,
        [((144, 128), F32)],
        [obs_weight] + sums,
        True,
        [pltpu.VMEM((CHUNK, 128), F32)],
        name="add_columns",
    )
    parts = swaps(part, "y")
    (pack,) = call(
        add_rows,
        [((8, PACK, 128), F32)],
        [ext] + parts,
        True,
        name="add_rows",
    )
    pack = lax.all_to_all(pack, "z", 0, 0, tiled=True)

    tall, centered, sent = ((80, 512), F32), ((128, 512), BF16), ((208, 128), BF16)
    blocks = [((512, 128), BF16), ((80, 512), BF16), ((512, 128), F32)]
    wide = pltpu.VMEM((128, 128), F32)
    work = [pltpu.VMEM((512, 512), F32), pltpu.VMEM((512, 512), BF16)]
    flops = 2 * 2 * 1024 * 128 * 512
    (g,) = call(
        first_batch,
        [sent],
        [pack, obs_value, obs_error_var],
        True,
        [pltpu.VMEM((80, 128), F32), wide],
        name="first_batch",
    )
    *both, loc = call(
        unpack,
        [tall] * 4 + [centered] * 4 + [((4, 32, 512), F32)],
        [pack, obs_index],
        True,
        flops=2 * 128 * 128 * 2048,
        name="unpack",
    )
    held = dict(enumerate(zip(both[:4], both[4:])))
    stacked = []
    beside = ((), ((1, 0), (2, 0)), ((2, 1), (3, 0)), ((3, 1), (3, 2)))
    for batch in range(4):
        news = {}
        for at, past in beside[batch]:
            news[at] = call(
                advance(at, past),
                [tall, centered],
                stacked[past] + [*news.get(at, held[at]), loc],
                False,
                work,
                flops=flops,
                name="advance",
            )
        own, other, flat = spread(g, [a for at in news for a in news[at]])
        for n, at in enumerate(news):
            held[at] = flat[2 * n : 2 * n + 2]
        at = min(batch, 3)
        part, *first = call(
            half(at, batch),
            [tall] + blocks * (batch < 3),
            own + [held[at][1], loc],
            True,
            work if batch < 3 else [pltpu.VMEM(s, d) for s, d in blocks] + work,
            flops=flops // 2,
            name="half",
        )
        if batch == 3:
            break
        g, *second = call(
            next_batch(batch + 1),
            [sent] + blocks,
            other + [*held[at], loc, part, obs_weight, obs_value, obs_error_var],
            True,
            work + [wide],
            flops=flops // 2,
            name="next_batch",
        )
        stacked.append(first + second)
    (state,) = call(
        finish,
        [tall],
        other + [*held[3], loc, part],
        True,
        [pltpu.VMEM(s, d) for s, d in blocks] + work + [pltpu.VMEM((80, 512), F32)],
        flops=flops // 2,
        name="finish",
    )
    return state


def solution(mesh):
    fine = Mesh(mesh.devices.reshape(8, 4, 4, 2), ("z", "y", "x", "c"))
    tiles = ("y", "x", "c")
    in_specs = (P("z", tiles), P(), P(), P(), P(), P(tiles + ("z",), None))
    out_specs = P(None, tiles + ("z",))
    return jax.shard_map(per_device, mesh=fine, in_specs=in_specs, out_specs=out_specs, check_vma=False)
```

```python
import jax
import jax.numpy as jnp
from jax import lax
from jax.experimental import pallas as pl
from jax.experimental.pallas import tpu as pltpu
from jax.sharding import Mesh, PartitionSpec as P

EPS = 1e-05
LOC_TABLE = (1.0, 0.6848958, 0.2083333, 0.0164931, 0.0)
F32 = jnp.float32
BF16 = jnp.bfloat16
VMEM = pl.BlockSpec(memory_space=pltpu.VMEM)

CHUNK = 168
PACK = 192


def place():
    z, y, x, c = [lax.axis_index(n) for n in ("z", "y", "x", "c")]
    block = x * 2 + c
    return [(y * 8 + block) * 4096, block, y, x, c, (y * 8 + block) * 32 + z * 4]


def call(body, shapes, args, placed=True, scratch=(), flops=0, name=None):
    outs = [jax.ShapeDtypeStruct(s, d) for s, d in shapes]
    moved = sum(a.size * a.dtype.itemsize for a in args) + sum(o.size * o.dtype.itemsize for o in outs)
    made = pl.pallas_call(
        (lambda *refs: body(place(), *refs)) if placed else body,
        out_shape=outs,
        in_specs=[VMEM] * len(args),
        out_specs=[VMEM] * len(outs),
        scratch_shapes=list(scratch),
        compiler_params=pltpu.CompilerParams(vmem_limit_bytes=16 * 2**20),
        cost_estimate=pl.CostEstimate(flops=flops, bytes_accessed=moved, transcendentals=0),
        name=name,
    )(*args)
    return list(made)


def lanes(info):
    return pl.ds(pl.multiple_of(info[1] * 128, 128), 128)


def pick(info, first_by, core, index_ref, ext_ref, tile, start_ref, out_refs):
    first = info[0]

    def group(n, carry):
        by = first_by ^ n
        block = (info[3] ^ by) * 2 + core
        here = pl.ds(pl.multiple_of(block * 128, 128), 128)
        for k in range(4):
            local = [index_ref[b, k : k + 1, here] - first for b in range(4)]
            tail = jnp.concatenate([jnp.broadcast_to(v, (2, 128)) for v in local], axis=0)
            wide = [jnp.broadcast_to(v, (8, 128)) for v in local] + [tail]
            for b in range(5):
                low = wide[b] & 127
                high = wide[b] >> 7
                top = 0 if b < 4 else 8
                rows = slice(40 * k + 8 * b, 40 * k + 8 * b + 8)
                acc = jnp.zeros((8, 128), F32) if start_ref is None else start_ref[by, rows, :]
                for part in range(32):
                    source = ext_ref[top : top + 8, part * 128 : (part + 1) * 128]
                    got = jnp.take_along_axis(source, low, axis=1)
                    acc = jnp.where(high == part, got, acc)
                out_refs[n, rows, :] = acc
        rest = tile if start_ref is None else tile + start_ref[by, 160:168, :]
        out_refs[n, 160:168, :] = rest
        return carry

    lax.fori_loop(0, out_refs.shape[0], group, 0)


def collect_other(info, index_ref, ens_ref, class_ref, out_ref, ext_ref, tile_ref, row_ref):
    ext_ref[0:8, :] = ens_ref[0:8, :]
    for r in range(4):
        ext_ref[8 + 2 * r : 10 + 2 * r, :] = ens_ref[8:10, :]
    even = lax.broadcasted_iota(jnp.int32, (32, 16), 0) == 2 * lax.broadcasted_iota(jnp.int32, (32, 16), 1)
    odd = lax.broadcasted_iota(jnp.int32, (32, 16), 0) == 2 * lax.broadcasted_iota(jnp.int32, (32, 16), 1) + 1
    mix = jnp.where(even, 1.0, jnp.where(odd, 8.0, 0.0)).astype(BF16)
    pairs = jnp.dot(class_ref[...].astype(F32).astype(BF16), mix, preferred_element_type=F32)
    for half in range(2):
        for i in range(4):
            row_ref[0:1, 64 * half + 16 * i : 64 * half + 16 * i + 16] = pairs[i : i + 1, :]
    row = lax.broadcasted_iota(jnp.int32, (8, 128), 0) == (info[2] & 1) * 4 + info[3]
    lane = (lax.broadcasted_iota(jnp.int32, (8, 128), 1) >> 6) == info[4]
    tile = jnp.where(row & lane, jnp.broadcast_to(row_ref[...], (8, 128)), 0.0)
    tile_ref[...] = tile
    pick(info, 0, 1 - info[4], index_ref, ext_ref, tile, None, out_ref)


def collect_own(info, index_ref, ext_ref, tile_ref, out_ref):
    pick(info, 2, info[4], index_ref, ext_ref, tile_ref[...], None, out_ref)


def collect_rest(info, index_ref, ext_ref, tile_ref, start_ref, p0_ref, p1_ref, work_ref):
    pick(info, 1, info[4], index_ref, ext_ref, tile_ref[...], start_ref, work_ref)
    p1_ref[...] = work_ref[0]
    p0_ref[...] = work_ref[1]


def add_cores(own_ref, other_ref, p2_ref, p3_ref):
    p2_ref[...] = own_ref[0] + other_ref[2]
    p3_ref[...] = own_ref[1] + other_ref[3]


def add_columns(info, weight_ref, p0_ref, p1_ref, p2_ref, p3_ref, out_ref, sum_ref):
    sum_ref[...] = (p0_ref[...] + p1_ref[...]) + (p2_ref[...] + p3_ref[...])
    here = lanes(info)
    head = jnp.zeros((8, 128), F32)
    tail = jnp.zeros((2, 128), F32)
    for k in range(4):
        weight = weight_ref[0, k : k + 1, here]
        head = head + sum_ref[40 * k : 40 * k + 8, :] * weight
        tail = tail + sum_ref[40 * k + 32 : 40 * k + 34, :] * weight
        out_ref[24 * k : 24 * k + 24, :] = sum_ref[40 * k + 8 : 40 * k + 32, :]
        out_ref[104 + 6 * k : 110 + 6 * k, :] = sum_ref[40 * k + 34 : 40 * k + 40, :]
    out_ref[96:104, :] = head
    out_ref[128:136, :] = jnp.zeros((8, 128), F32)
    out_ref[128:130, :] = tail
    out_ref[136:144, :] = sum_ref[160:168, :]


def add_rows(info, ext_ref, p0_ref, p1_ref, p2_ref, p3_ref, out_ref):
    parts = [p0_ref, p1_ref, p2_ref, p3_ref]
    total = (p0_ref[0:136, :] + p1_ref[0:136, :]) + (p2_ref[0:136, :] + p3_ref[0:136, :])
    classes = [jnp.zeros((8, 128), F32)] * 2
    for s in range(4):
        upper = (info[2] ^ s) >> 1
        for t in range(2):
            classes[t] = classes[t] + jnp.where(upper == t, parts[s][136:144, :], 0.0)
    pair = lax.broadcasted_iota(jnp.int32, (8, 128), 0) >> 1
    for z in range(8):
        out_ref[z, 0:136, :] = total
        last = jnp.zeros((8, 128), F32)
        for i in range(4):
            at = slice(512 * z + 128 * i, 512 * z + 128 * i + 128)
            out_ref[z, 136 + 8 * i : 144 + 8 * i, :] = ext_ref[0:8, at]
            last = jnp.where(pair == i, ext_ref[8:16, at], last)
        out_ref[z, 168:176, :] = last
        for t in range(2):
            out_ref[z, 176 + 8 * t : 184 + 8 * t, :] = classes[t]


def increments(prior, value, errvar, out_ref, wide_ref):
    mean = jnp.mean(prior, axis=0, keepdims=True)
    anom = prior - mean
    var = jnp.sum(anom * anom, axis=0, keepdims=True) / 79.0
    inverse = 1.0 / (var + EPS)
    post_var = 1.0 / (inverse + 1.0 / errvar)
    post_mean = post_var * (mean * inverse + value / errvar)
    shrink = jnp.sqrt(errvar / (errvar + var))
    incr = post_mean - mean + (shrink - 1.0) * anom
    rest = inverse / 79.0
    wide_ref[0:80, :] = anom.astype(BF16).astype(F32)
    wide_ref[80:128, :] = jnp.zeros((48, 128), F32)
    for row in (80, 81, 82):
        part = rest.astype(BF16).astype(F32)
        wide_ref[row : row + 1, :] = part
        rest = rest - part
    out_ref[0:128, :] = jnp.transpose(wide_ref[...]).astype(BF16)
    out_ref[128:208, :] = incr.astype(BF16)


def first_batch(info, pack_ref, value_ref, errvar_ref, out_ref, prior_ref, wide_ref):
    for z in range(8):
        prior_ref[8 * z : 8 * z + 8, :] = pack_ref[z, 96:104, :]
        prior_ref[64 + 2 * z : 66 + 2 * z, :] = pack_ref[z, 128:130, :]
    here = lanes(info)
    increments(prior_ref[...], value_ref[0:1, here], errvar_ref[0:1, here], out_ref, wide_ref)


def center(x, out_ref):
    out_ref[0:80, :] = (x - jnp.mean(x, axis=0, keepdims=True)).astype(BF16)
    out_ref[80:128, :] = jnp.zeros((48, x.shape[1]), BF16)


def unpack(info, pack_ref, index_ref, *refs):
    outs, centered, loc_ref = refs[:4], refs[4:8], refs[8]
    here = lanes(info)
    table = pack_ref[:, 176:192, :].reshape(128, 128).astype(BF16)
    for b in range(4):
        for k in range(4):
            at = slice(128 * k, 128 * k + 128)
            for z in range(8):
                if b < 3:
                    outs[b][8 * z : 8 * z + 8, at] = pack_ref[z, 24 * k + 8 * b : 24 * k + 8 * b + 8, :]
                    outs[b][64 + 2 * z : 66 + 2 * z, at] = pack_ref[z, 104 + 6 * k + 2 * b : 106 + 6 * k + 2 * b, :]
                else:
                    outs[b][8 * z : 8 * z + 8, at] = pack_ref[z, 136 + 8 * k : 144 + 8 * k, :]
                    outs[b][64 + 2 * z : 66 + 2 * z, at] = pack_ref[z, 168 + 2 * k : 170 + 2 * k, :]
            if b < 3:
                block = index_ref[b + 1, k : k + 1, here] >> 7
            else:
                block = jnp.full((1, 128), info[5] + k, jnp.int32)
            holder = ((block >> 2) & 7) * 16 + (block >> 6)
            own = (lax.broadcasted_iota(jnp.int32, (128, 128), 0) == holder).astype(F32).astype(BF16)
            found = lax.dot_general(table, own, (((0,), (0,)), ((), ())), preferred_element_type=F32)
            which = ((block >> 5) & 1) * 4 + (block & 3)
            pairs = jnp.zeros((16, 128), F32)
            for i in range(8):
                pairs = pairs + jnp.where(which == i, found[16 * i : 16 * i + 16, :], 0.0)
            odd = jnp.floor(pairs * 0.125)
            for core, level in ((info[4], pairs - 8.0 * odd), (1 - info[4], odd)):
                weights = jnp.zeros((16, 128), F32)
                for n, w in enumerate(LOC_TABLE):
                    weights = weights + jnp.where(level == n, w, 0.0)
                loc_ref[b, pl.ds(pl.multiple_of(core * 16, 16), 16), at] = weights
    for x_ref, c_ref in zip(outs, centered):
        center(x_ref[...], c_ref)


def stack(info, refs, anom_ref, incr_ref, inverse_ref):
    for s, ref in enumerate(refs):
        at = pl.ds(pl.multiple_of((info[3] ^ s) * 128, 128), 128)
        anom_ref[at, :] = ref[0:128, :]
        incr_ref[:, at] = ref[128:208, :]
    lane = lax.broadcasted_iota(jnp.int32, (128, 128), 0)
    parts = jnp.where((lane >= 80) & (lane < 83), 1.0, 0.0).astype(BF16)
    inverse_ref[...] = jnp.dot(anom_ref[...], parts, preferred_element_type=F32)


def change(other, centered_ref, loc_ref, at, batch, anom_ref, incr_ref, inverse_ref, cov_ref, gain_ref):
    cov_ref[...] = jnp.dot(anom_ref[...], centered_ref[...], preferred_element_type=F32)
    for p in range(4):
        row = 16 * other + 4 * batch + p
        rows = slice(128 * p, 128 * p + 128)
        for k in range(4):
            cols = slice(128 * k, 128 * k + 128)
            gain_ref[rows, cols] = ((cov_ref[rows, cols] * inverse_ref[rows, :]) * loc_ref[at, row : row + 1, cols]).astype(BF16)
    return jnp.dot(incr_ref[...], gain_ref[...], preferred_element_type=F32)


def half(at, batch):
    def body(info, *refs):
        c_ref, loc_ref, part_ref, anom_ref, incr_ref, inverse_ref, cov_ref, gain_ref = refs[4:]
        stack(info, refs[:4], anom_ref, incr_ref, inverse_ref)
        part_ref[...] = change(0, c_ref, loc_ref, at, batch, anom_ref, incr_ref, inverse_ref, cov_ref, gain_ref)

    return body


def next_batch(batch):
    def body(info, *refs):
        x_ref, c_ref, loc_ref, part_ref, weight_ref, value_ref, errvar_ref = refs[4:11]
        out_ref, anom_ref, incr_ref, inverse_ref, cov_ref, gain_ref, wide_ref = refs[11:]
        stack(info, refs[:4], anom_ref, incr_ref, inverse_ref)
        blocks = (anom_ref, incr_ref, inverse_ref, cov_ref, gain_ref)
        x = x_ref[...] + (part_ref[...] + change(1, c_ref, loc_ref, batch - 1, batch - 1, *blocks))
        here = lanes(info)
        prior = x[:, 0:128] * weight_ref[batch, 0:1, here]
        for k in range(1, 4):
            prior = prior + x[:, 128 * k : 128 * k + 128] * weight_ref[batch, k : k + 1, here]
        increments(prior, value_ref[batch : batch + 1, here], errvar_ref[batch : batch + 1, here], out_ref, wide_ref)

    return body


def advance(at, batch):
    def body(*refs):
        own, other = refs[:3], refs[3:6]
        x_ref, c_ref, loc_ref, out_ref, c_out_ref, cov_ref, gain_ref = refs[6:]
        first = change(0, c_ref, loc_ref, at, batch, *own, cov_ref, gain_ref)
        x = x_ref[...] + (first + change(1, c_ref, loc_ref, at, batch, *other, cov_ref, gain_ref))
        out_ref[...] = x
        center(x, c_out_ref)

    return body


def finish(info, *refs):
    x_ref, c_ref, loc_ref, part_ref, out_ref, anom_ref, incr_ref, inverse_ref, cov_ref, gain_ref, work_ref = refs[4:]
    stack(info, refs[:4], anom_ref, incr_ref, inverse_ref)
    blocks = (anom_ref, incr_ref, inverse_ref, cov_ref, gain_ref)
    work_ref[...] = x_ref[...] + (part_ref[...] + change(1, c_ref, loc_ref, 3, 3, *blocks))
    for z in range(8):
        out_ref[10 * z : 10 * z + 8, :] = work_ref[8 * z : 8 * z + 8, :]
        out_ref[10 * z + 8 : 10 * z + 10, :] = work_ref[64 + 2 * z : 66 + 2 * z, :]


def swap(a, axis, by, size):
    return lax.ppermute(a, axis, [(i, i ^ by) for i in range(size)])


def swaps(a, axis):
    got = {s: swap(a, axis, s, 4) for s in (1, 3, 2)}
    return [a, got[1], got[2], got[3]]


def spread(g, beside=()):
    own = swaps(g, "x")
    if beside:
        own[2], *beside = lax.optimization_barrier((own[2], *beside))
    return own, [swap(v, "c", 1, 2) for v in own], list(beside)


def per_device(ensemble, obs_index, obs_weight, obs_value, obs_error_var, loc_class):
    rows = [((CHUNK, 128), F32)]
    other, ext, tile = call(
        collect_other,
        [((4, CHUNK, 128), F32), ((16, 4096), F32), ((8, 128), F32)],
        [obs_index, ensemble, loc_class],
        True,
        [pltpu.VMEM((1, 128), F32)],
        name="collect_other",
    )
    other = swap(other, "c", 1, 2)
    (own,) = call(collect_own, [((2, CHUNK, 128), F32)], [obs_index, ext, tile], True, flops=10**9, name="collect_own")
    p2, p3 = call(add_cores, rows * 2, [own, other], False, name="add_cores")
    p2, p3 = swap(p2, "x", 2, 4), swap(p3, "x", 3, 4)
    p0, p1 = call(
        collect_rest,
        rows * 2,
        [obs_index, ext, tile, other],
        True,
        [pltpu.VMEM((2, CHUNK, 128), F32)],
        flops=10**9,
        name="collect_rest",
    )
    sums = [p0, swap(p1, "x", 1, 4), p2, p3]
    (part,) = call(
        add_columns,
        [((144, 128), F32)],
        [obs_weight] + sums,
        True,
        [pltpu.VMEM((CHUNK, 128), F32)],
        name="add_columns",
    )
    parts = swaps(part, "y")
    (pack,) = call(
        add_rows,
        [((8, PACK, 128), F32)],
        [ext] + parts,
        True,
        name="add_rows",
    )
    pack = lax.all_to_all(pack, "z", 0, 0, tiled=True)

    tall, centered, sent = ((80, 512), F32), ((128, 512), BF16), ((208, 128), BF16)
    blocks = [((512, 128), BF16), ((80, 512), BF16), ((512, 128), F32)]
    wide = pltpu.VMEM((128, 128), F32)
    work = [pltpu.VMEM((512, 512), F32), pltpu.VMEM((512, 512), BF16)]
    flops = 2 * 2 * 1024 * 128 * 512
    (g,) = call(
        first_batch,
        [sent],
        [pack, obs_value, obs_error_var],
        True,
        [pltpu.VMEM((80, 128), F32), wide],
        name="first_batch",
    )
    *both, loc = call(
        unpack,
        [tall] * 4 + [centered] * 4 + [((4, 32, 512), F32)],
        [pack, obs_index],
        True,
        flops=2 * 128 * 128 * 2048,
        name="unpack",
    )
    stacked = []
    beside = ((), ((1, 0), (2, 0)), ((2, 1), (3, 0)), ((3, 1), (3, 2)))
    for batch in range(4):
        news = {}
        for at, past in beside[batch]:
            news[at] = call(
                advance(at, past),
                [tall, centered],
                stacked[past] + [*news.get(at, held[at]), loc],
                False,
                work,
                flops=flops,
                name="advance",
            )
        if batch == 0:
            own, other, (*both, loc) = spread(g, [*both, loc])
            held = dict(enumerate(zip(both[:4], both[4:])))
        else:
            own, other, flat = spread(g, [a for at in news for a in news[at]])
        for n, at in enumerate(news):
            held[at] = flat[2 * n : 2 * n + 2]
        at = min(batch, 3)
        part, *first = call(
            half(at, batch),
            [tall] + blocks * (batch < 3),
            own + [held[at][1], loc],
            True,
            work if batch < 3 else [pltpu.VMEM(s, d) for s, d in blocks] + work,
            flops=flops // 2,
            name="half",
        )
        if batch == 3:
            break
        g, *second = call(
            next_batch(batch + 1),
            [sent] + blocks,
            other + [*held[at], loc, part, obs_weight, obs_value, obs_error_var],
            True,
            work + [wide],
            flops=flops // 2,
            name="next_batch",
        )
        stacked.append(first + second)
    (state,) = call(
        finish,
        [tall],
        other + [*held[3], loc, part],
        True,
        [pltpu.VMEM(s, d) for s, d in blocks] + work + [pltpu.VMEM((80, 512), F32)],
        flops=flops // 2,
        name="finish",
    )
    return state


def solution(mesh):
    fine = Mesh(mesh.devices.reshape(8, 4, 4, 2), ("z", "y", "x", "c"))
    tiles = ("y", "x", "c")
    in_specs = (P("z", tiles), P(), P(), P(), P(), P(tiles + ("z",), None))
    out_specs = P(None, tiles + ("z",))
    return jax.shard_map(per_device, mesh=fine, in_specs=in_specs, out_specs=out_specs, check_vma=False)
```
